512 devices in a mesh: dp: 64 (over y, z), fsdp: 8 (over x, core).
Axes of the slice: x: 4, y: 4, z: 16, core: 2. Of those that a mesh axis runs over, the one named last changes fastest.
Arguments:
- gradient: float32 [64, 3072, 1024], P('dp', 'fsdp'), may hold values from -64 to 64
- residual: float32 [64, 3072, 1024], P('dp', 'fsdp'), may hold values from -3 to 3
- sign_flips: int32 [3072, 1024], P('fsdp'), may hold values from -1 to 1, as said below
- level_table: int32 [16], replicated, may hold values from 0 to 124, as said below
Outputs:
- mean_gradient: float32 [3072, 1024], P('fsdp')
- new_residual: float32 [64, 3072, 1024], P('dp', 'fsdp')
The draws below stay inside these ranges and needn't reach their ends.
Inputs may be any that keep to these rules, and one draw needn't show every extreme that they name: `sign_flips`: each entry is -1 or 1. `level_table`: first entry 0, last entry 124, strictly increasing, consecutive entries differ by 4 to 12.
All inputs are finite; a program needn't handle non-finite values. Where the reference program divides by a largest or mean magnitude, that divisor is 1e-20 or more.
Results may differ from the reference program's by a relative error of at most 0.0028.
Values may be sent and summed in bfloat16 or wider, within the bound.
No kernel may reach another device: no remote copies, remote signals or barrier semaphores. Data moves between devices by JAX's collectives and lax.ppermute only.
A program may use at most 64 MiB of HBM per device.

```python
import math
import jax
import jax.numpy as jnp
from jax import lax

BLK = 1024
LEVELS = 16
NBLK = 3072
N_DP = 64


def draw_sign_flips(key, part):
    key = jax.random.fold_in(key, 11)
    coins = jax.random.randint(key, (NBLK, BLK), 0, 2)
    return (2 * coins - 1).astype(jnp.int32)


def draw_level_table(key, part):
    key = jax.random.fold_in(key, 23)
    spacing_set = jnp.array([4, 5, 6, 7, 8, 9, 10, 11, 12, 4, 6, 8, 10, 12, 12], jnp.int32)
    spacing = jax.random.permutation(key, spacing_set)
    return jnp.concatenate([jnp.zeros((1,), jnp.int32), jnp.cumsum(spacing).astype(jnp.int32)])


def spiked(entries, stream_key, source, target, blocks, factor):
    owner, partner = [(jnp.arange(entries.shape[axis_at]) // (entries.shape[axis_at] // blocks)).reshape([-1 if axis == axis_at else 1 for axis in range(entries.ndim)]) for axis_at in (source, target)]
    chosen = jax.random.permutation(stream_key, blocks)[partner]
    strong = (owner == chosen) | (owner == (partner + blocks // 2) % blocks)
    return jnp.where(strong, factor * entries, entries)


def steps_of(stream_key, extent, split, smallest, largest):
    factor_of = 1.0
    for axis_at, blocks in split:
        draws = jax.random.uniform(jax.random.fold_in(jax.random.fold_in(stream_key, 6), axis_at), (blocks,), jnp.float32, smallest / len(split), largest / len(split))
        factor_of = factor_of * jnp.repeat(jnp.exp(draws), extent[axis_at] // blocks).reshape((-1,) + (1,) * (len(extent) - 1 - axis_at))
    return factor_of


def scatter_about(own_key, dims, scale, most, pieces=(), kind=jnp.bfloat16):
    gain = steps_of(own_key, dims, pieces, -0.22, 0.18) if pieces else 1.0
    drawn = jax.random.normal(own_key, dims, jnp.float32) * scale * gain
    return jnp.minimum(jnp.maximum(drawn, -most), most).astype(kind)


def noise_with(rng, shape, scale, reach, shards, heavy, kind=jnp.bfloat16):
    values = scale * jax.random.normal(rng, shape, jnp.float32)
    if shards:
        values = values * steps_of(rng, shape, shards, -0.22, 0.18)
    return jnp.clip(spiked(values, jax.random.fold_in(rng, 3), *heavy), -reach, reach).astype(kind)


def setup_inputs(seed: int = 0) -> dict:
    arg_keys = jax.random.split(jax.random.key(seed), 5)
    gradient = noise_with(arg_keys[0], (N_DP, NBLK, BLK), 4.0, 64.0, ((0, 64), (1, 8)), (0, 1, 64, 4.0), jnp.float32)
    residual = scatter_about(arg_keys[1], (N_DP, NBLK, BLK), 0.5, 3.0, ((0, 64), (1, 8)), jnp.float32)
    sign_flips = draw_sign_flips(jax.random.fold_in(arg_keys[4], 71), 0)
    level_table = draw_level_table(jax.random.fold_in(arg_keys[4], 71), 0)
    return {"gradient": gradient, "residual": residual, "sign_flips": sign_flips, "level_table": level_table}


def walsh(values):
    width = values.shape[-1]
    lead = values.shape[:-1]
    step = 1
    while step < width:
        folded = values.reshape(lead + (width // (2 * step), 2, step))
        first = folded[..., 0, :]
        second = folded[..., 1, :]
        values = jnp.stack([first + second, first - second], axis=-2).reshape(lead + (width,))
        step = step * 2
    return values

def soft_code(offset, centred):
    numer = jnp.zeros_like(offset)
    denom = jnp.zeros_like(offset)
    for level in range(LEVELS):
        gap = offset - centred[level]
        weight = jnp.exp(-gap * gap / 72.0)
        numer = numer + weight * centred[level]
        denom = denom + weight
    return numer / denom

def reference(gradient, residual, sign_flips, level_table):
    flips = sign_flips.astype(jnp.float32)
    levels = level_table.astype(jnp.float32)
    bottom = levels[0]
    upper = levels[LEVELS - 1]
    middle = (bottom + upper) / 2.0
    half_span = (upper - bottom) / 2.0
    centred = levels - middle
    root = math.sqrt(BLK)

    def turn(pair):
        grad_rows, resid_rows = pair
        return walsh(grad_rows * flips) / root + resid_rows
    rotated = lax.map(turn, (gradient, residual))
    peak_value = jnp.max(jnp.abs(rotated)) + 1e-06

    def quantize(rows):
        code_full = soft_code(rows * half_span / peak_value, centred)
        return (rows - code_full * peak_value / half_span, code_full.astype(jnp.bfloat16))
    new_residual, codes = lax.map(quantize, rotated)
    total = lax.optimization_barrier(jnp.sum(codes, axis=0, dtype=jnp.float32))
    mean_gradient = walsh(total * peak_value / (half_span * N_DP)) / root * flips
    return (mean_gradient, new_residual)
```

```python
import functools
import math

import jax
import jax.numpy as jnp
import numpy as np
from jax import lax
from jax.experimental import pallas as pl
from jax.experimental.pallas import tpu as pltpu
from jax.sharding import PartitionSpec as P

F32, BF16, F16 = jnp.float32, jnp.bfloat16, jnp.float16
FOLD = 256
LANES = 128
VMEM_BYTES = 48 * 1024 * 1024


def hadamard(width):
    table = np.ones((1, 1), np.float32)
    while table.shape[0] < width:
        table = np.block([[table, table], [table, -table]])
    return table


def turn(values, matrix, scale):
    count = values.shape[1] // FOLD
    parts = [values[:, k * FOLD : (k + 1) * FOLD] for k in range(count)]
    step = 1
    while step < count:
        nxt = list(parts)
        for k in range(count):
            if not k & step:
                nxt[k] = parts[k] + parts[k + step]
                nxt[k + step] = parts[k] - parts[k + step]
        parts = nxt
        step *= 2
    turned = []
    for part in parts:
        part = part * scale
        high = part.astype(BF16)
        rest = part - high.astype(F32)
        middle = rest.astype(BF16)
        low = (rest - middle.astype(F32)).astype(BF16)
        dot = functools.partial(jnp.dot, preferred_element_type=F32)
        turned.append(dot(high, matrix) + (dot(middle, matrix) + dot(low, matrix)))
    return turned


def rotate_kernel(copies, grad_ref, flip_ref, resid_ref, matrix_ref, rot_ref, peak_ref):
    width = grad_ref.shape[1]
    signed = grad_ref[...] * flip_ref[...].astype(F32)
    turned = turn(signed, matrix_ref[...], 1.0 / math.sqrt(width))
    top = jnp.zeros((8, LANES), F32)
    for k, part in enumerate(turned):
        cols = slice(k * FOLD, (k + 1) * FOLD)
        rotated = part + resid_ref[:, cols]
        rot_ref[:, cols] = rotated
        size = jnp.abs(rotated)
        for at in range(0, FOLD, LANES):
            lane = size[:, at : at + LANES]
            top = jnp.maximum(top, jnp.max(lane.reshape(-1, 8, LANES), axis=0))
    top = jnp.broadcast_to(top[None], (copies, 8, LANES))

    @pl.when(pl.program_id(0) == 0)
    def _():
        peak_ref[...] = top

    @pl.when(pl.program_id(0) > 0)
    def _():
        peak_ref[...] = jnp.maximum(peak_ref[...], top)


def quantize_kernel(levels_ref, peaks_ref, rot_ref, resid_ref, code_ref, peak_ref):
    count = levels_ref.shape[0]
    peak = jnp.max(peaks_ref[...]) + 1e-06
    bottom = levels_ref[0].astype(F32)
    upper = levels_ref[count - 1].astype(F32)
    middle = (bottom + upper) * 0.5
    half_span = (upper - bottom) * 0.5
    log2e = math.log2(math.e)
    centred = [levels_ref[k].astype(F32) - middle for k in range(count)]
    lift = [c * c * (-log2e / 72.0) for c in centred]
    peak_row = jnp.full((1, LANES), peak, F32)
    half_row = jnp.full((1, LANES), half_span, F32)
    reach = half_row / peak_row
    back = peak_row / half_row
    reach = reach[0:1, 0:1] * (log2e / 36.0)
    back = back[0:1, 0:1]
    peak_ref[...] = jnp.full(peak_ref.shape, peak, F32)
    rows, width = rot_ref.shape
    wide = 512
    per_row = width // wide

    def chunk(step, carry):
        row = pl.multiple_of((step // per_row) * 16, 16)
        col = pl.multiple_of((step % per_row) * wide, wide)
        at = (pl.ds(row, 16), pl.ds(col, wide))
        rotated = rot_ref[at]
        place = rotated * reach
        numer = jnp.zeros_like(place)
        denom = jnp.zeros_like(place)
        for k in range(count):
            weight = jnp.exp2(place * centred[k] + lift[k])
            numer = numer + weight * centred[k]
            denom = denom + weight
        code = numer / denom
        resid_ref[at] = rotated - code * back
        code_ref[at] = code.astype(BF16)
        return carry

    lax.fori_loop(0, (rows // 16) * per_row, chunk, 0)


def partial_kernel(codes_ref, matrix_ref, out_ref):
    width = codes_ref.shape[2]
    total = codes_ref[0].astype(F32)
    for k in range(1, codes_ref.shape[0]):
        total = total + codes_ref[k].astype(F32)
    turned = turn(total, matrix_ref[...], 1.0 / math.sqrt(width))
    for k, part in enumerate(turned):
        for at in range(0, FOLD, LANES):
            out_ref[(k * FOLD + at) // LANES] = part[:, at : at + LANES]


def on_device(gradient, residual, sign_flips, level_table):
    _, rows, width = gradient.shape
    replicas = lax.axis_size("dp")
    parts = lax.axis_size("fsdp")
    depth = 16
    ys = replicas // depth
    near = [[y * depth + 2 * h + l for y in range(ys) for l in range(2)] for h in range(depth // 2)]
    far = [[y * depth + 2 * h + l for h in range(depth // 2)] for y in range(ys) for l in range(2)]
    along_y = [[y * depth + z for y in range(ys)] for z in range(depth)]
    along_z = [[y * depth + z for z in range(depth)] for y in range(ys)]
    matrix = jnp.asarray(hadamard(FOLD), BF16)
    params = functools.partial(pltpu.CompilerParams, vmem_limit_bytes=VMEM_BYTES)

    block = 96
    tile = pl.BlockSpec((block, width), lambda i: (i, 0))
    whole = lambda *shape: pl.BlockSpec(shape, lambda i: (0,) * len(shape))
    rotated, peaks = pl.pallas_call(
        functools.partial(rotate_kernel, parts),
        grid=(rows // block,),
        in_specs=[tile, tile, tile, whole(FOLD, FOLD)],
        out_specs=[tile, whole(parts, 8, LANES)],
        out_shape=[
            jax.ShapeDtypeStruct((rows, width), F32),
            jax.ShapeDtypeStruct((parts, 8, LANES), F32),
        ],
        compiler_params=params(),
        name="rotate",
    )(gradient[0], sign_flips, residual[0], matrix)

    def spread(tiles, axis, groups, size):
        top = jnp.max(tiles, axis=0, keepdims=True)
        return lax.all_to_all(
            jnp.broadcast_to(top, (size, 8, LANES)), axis, 0, 0, axis_index_groups=groups
        )

    peaks = lax.all_to_all(peaks, "fsdp", 0, 0)
    peaks = spread(peaks, "dp", along_y, ys)
    peaks = spread(peaks, "dp", along_z, depth)

    new_residual, codes, peak = pl.pallas_call(
        quantize_kernel,
        grid=(rows // block,),
        in_specs=[
            pl.BlockSpec(memory_space=pltpu.SMEM),
            whole(depth, 8, LANES),
            tile,
        ],
        out_specs=[tile, tile, whole(1, LANES)],
        out_shape=[
            jax.ShapeDtypeStruct((rows, width), F32),
            jax.ShapeDtypeStruct((rows, width), BF16),
            jax.ShapeDtypeStruct((1, LANES), F32),
        ],
        compiler_params=params(),
        name="quantize",
    )(level_table, peaks, rotated)

    first, second = len(near[0]), len(far[0])
    share = rows // first
    codes = codes.reshape(first, share, width)
    codes = lax.all_to_all(codes, "dp", 0, 0, axis_index_groups=near)
    partial = pl.pallas_call(
        partial_kernel,
        out_shape=jax.ShapeDtypeStruct((second, share, width // second), F32),
        compiler_params=params(),
        name="partial",
    )(codes, matrix)
    partial = lax.all_to_all(partial.astype(F16), "dp", 0, 0, axis_index_groups=far)
    mean = jnp.sum(partial.astype(F32), axis=0) * 0.125
    mean = jnp.broadcast_to(mean.astype(F16)[None], partial.shape)
    mean = lax.all_to_all(mean, "dp", 0, 0, axis_index_groups=far)
    mean = mean.transpose(1, 0, 2).reshape(share, width)
    mean = jnp.broadcast_to(mean[None], (first, share, width))
    mean = lax.all_to_all(mean, "dp", 0, 0, axis_index_groups=near)
    half_span = (level_table[-1] - level_table[0]).astype(F32) * 0.5
    factor = peak[0, 0] / (half_span * (replicas // 8))
    mean = mean.reshape(rows, width).astype(F32) * factor * sign_flips.astype(F32)
    return mean, new_residual[None]


def solution(mesh):
    placed = (P("dp", "fsdp", None), P("dp", "fsdp", None), P("fsdp", None), P())
    return jax.shard_map(
        on_device,
        mesh=mesh,
        in_specs=placed,
        out_specs=(P("fsdp", None), P("dp", "fsdp", None)),
        check_vma=False,
    )
```

```python
import functools
import math

import jax
import jax.numpy as jnp
from jax import lax
from jax.experimental import pallas as pl
from jax.experimental.pallas import tpu as pltpu
from jax.sharding import PartitionSpec as P

F32, BF16, F16 = jnp.float32, jnp.bfloat16, jnp.float16
FOLD = 256
LANES = 128
VMEM_BYTES = 32 * 1024 * 1024
ROTATE_BYTES = 52 * 1024 * 1024
LOG2E = math.log2(math.e)


def hadamard(width):
    row = lax.broadcasted_iota(jnp.int32, (width, width), 0)
    col = lax.broadcasted_iota(jnp.int32, (width, width), 1)
    common = row & col
    step = 1
    while step < width.bit_length():
        common = common ^ (common >> step)
        step *= 2
    return (1 - 2 * (common & 1)).astype(F32).astype(BF16)


def turn(values, matrix, scale):
    count = values.shape[1] // FOLD
    parts = [values[:, k * FOLD : (k + 1) * FOLD] for k in range(count)]
    step = 1
    while step < count:
        nxt = list(parts)
        for k in range(count):
            if not k & step:
                nxt[k] = parts[k] + parts[k + step]
                nxt[k + step] = parts[k] - parts[k + step]
        parts = nxt
        step *= 2
    turned = []
    for part in parts:
        part = part * scale
        high = part.astype(BF16)
        rest = part - high.astype(F32)
        middle = rest.astype(BF16)
        low = (rest - middle.astype(F32)).astype(BF16)
        dot = functools.partial(jnp.dot, preferred_element_type=F32)
        turned.append(dot(high, matrix) + (dot(middle, matrix) + dot(low, matrix)))
    return turned


def rotate_kernel(
    grad_hbm, flip_hbm, resid_hbm, rot_ref, peak_ref, matrix_ref,
    grad, flip, resid, sems,
):
    rows, width = rot_ref.shape
    chunks = sems.shape[0]
    deep = rows // chunks
    copies = []
    for c in range(chunks):
        at = pl.ds(c * deep, deep)
        copies.append([])
        for k, (src, dst) in enumerate(((grad_hbm, grad), (flip_hbm, flip), (resid_hbm, resid))):
            copies[c].append(pltpu.make_async_copy(src.at[at], dst.at[at], sems.at[c, k]))
            copies[c][k].start()

    matrix_ref[...] = hadamard(FOLD)

    top = jnp.zeros((8, LANES), F32)
    for c in range(chunks):
        for copy in copies[c]:
            copy.wait()
        at = slice(c * deep, (c + 1) * deep)
        signed = grad[at, :] * flip[at, :].astype(F32)
        for k, part in enumerate(turn(signed, matrix_ref[...], 1.0 / math.sqrt(width))):
            cols = slice(k * FOLD, (k + 1) * FOLD)
            rotated = part + resid[at, cols]
            rot_ref[at, cols] = rotated
            size = jnp.abs(rotated)
            for lane in range(0, FOLD, LANES):
                tiles = size[:, lane : lane + LANES].reshape(-1, 8, LANES)
                top = jnp.maximum(top, jnp.max(tiles, axis=0))
    peak_ref[...] = jnp.broadcast_to(jnp.max(top, axis=0, keepdims=True), peak_ref.shape)


def table_kernel(level_ref, centre_ref, lift_ref):
    count = level_ref.shape[0]
    bottom = level_ref[0].astype(F32)
    upper = level_ref[count - 1].astype(F32)
    middle = (bottom + upper) * 0.5
    for k in range(count):
        centred = jnp.full((8, LANES), level_ref[k].astype(F32) - middle, F32)
        centre_ref[k] = centred
        lift_ref[k] = centred * centred * (-LOG2E / 72.0)


def quantize_kernel(replicas, peaks_ref, rot_ref, centre_ref, lift_ref, code_ref, full_ref, scale_ref, factor_ref):
    count = centre_ref.shape[0]
    rows, width = rot_ref.shape
    top = jnp.max(peaks_ref[...], axis=0, keepdims=True)
    peak = jnp.max(top, axis=1, keepdims=True) + 1e-06
    peak = jnp.broadcast_to(peak, (8, LANES))
    half_span = (centre_ref[count - 1] - centre_ref[0]) * 0.5
    scale = peak / half_span
    scale_ref[...] = scale
    factor_ref[...] = jnp.tile(scale[0:1] * (8.0 / replicas), (1, width // LANES))
    reach = half_span / peak * (LOG2E / 36.0)
    groups = [(r, slice(l * LANES, (l + 1) * LANES)) for l in range(width // LANES) for r in range(2)]

    def chunk(step, carry):
        row = pl.multiple_of(step * 16, 16)
        place = [rot_ref[pl.ds(row + 8 * r, 8), l] * reach for r, l in groups]
        numer, denom = [None] * len(groups), [None] * len(groups)
        for k in range(count):
            centred, lift = centre_ref[k], lift_ref[k]
            for i in range(len(groups)):
                weight = jnp.exp2(place[i] * centred + lift)
                moment = weight * centred
                numer[i] = moment if k == 0 else numer[i] + moment
                denom[i] = weight if k == 0 else denom[i] + weight
        for i in range(0, len(groups), 2):
            code = jnp.concatenate([numer[i] / denom[i], numer[i + 1] / denom[i + 1]], axis=0)
            full_ref[pl.ds(row, 16), groups[i][1]] = code
            code_ref[pl.ds(row, 16), groups[i][1]] = code.astype(BF16)
        return carry

    lax.fori_loop(0, rows // 16, chunk, 0)


def residual_kernel(rot_ref, full_ref, scale_ref, out_ref):
    scale = scale_ref[0:1, 0:1]
    out_ref[...] = rot_ref[...] - full_ref[...] * scale


def partial_kernel(codes_ref, matrix_ref, out_ref):
    width = codes_ref.shape[2]
    total = codes_ref[0].astype(F32)
    for k in range(1, codes_ref.shape[0]):
        total = total + codes_ref[k].astype(F32)
    turned = turn(total, matrix_ref[...], 1.0 / math.sqrt(width))
    for k, part in enumerate(turned):
        for at in range(0, FOLD, LANES):
            out_ref[(k * FOLD + at) // LANES] = part[:, at : at + LANES]


def grouped(pieces, axes, groups):
    return lax.all_to_all(pieces, axes, 0, 0, axis_index_groups=groups)


def on_device(gradient, residual, sign_flips, level_table):
    _, rows, width = gradient.shape
    levels = level_table.shape[0]
    replicas, splits = lax.axis_size("dp"), lax.axis_size("fsdp")
    depth = 16
    ys, pairs = range(replicas // depth), range(depth // 2)
    near = [[y * depth + 2 * h + l for y in ys for l in range(2)] for h in pairs]
    far = [[y * depth + 2 * h + l for h in pairs] for y in ys for l in range(2)]
    line = [[y * depth + z for z in range(depth)] for y in ys]
    plane = [[(y * depth + z) * splits + f for y in ys for f in range(splits)] for z in range(depth)]
    params = functools.partial(pltpu.CompilerParams, vmem_limit_bytes=VMEM_BYTES)
    hbm, vmem = pl.BlockSpec(memory_space=pltpu.HBM), pl.BlockSpec(memory_space=pltpu.VMEM)
    like = jax.ShapeDtypeStruct

    chunks = 4
    rotated, peaks, matrix = pl.pallas_call(
        rotate_kernel,
        in_specs=[hbm] * 3,
        out_specs=[vmem] * 3,
        out_shape=[
            like((rows, width), F32),
            like((len(plane[0]), LANES), F32),
            like((FOLD, FOLD), BF16),
        ],
        scratch_shapes=[
            pltpu.VMEM((rows, width), F32),
            pltpu.VMEM((rows, width), jnp.int32),
            pltpu.VMEM((rows, width), F32),
            pltpu.SemaphoreType.DMA((chunks, 3)),
        ],
        compiler_params=pltpu.CompilerParams(vmem_limit_bytes=ROTATE_BYTES),
        name="rotate",
    )(gradient[0], sign_flips, residual[0])
    centred, lift = pl.pallas_call(
        table_kernel,
        in_specs=[pl.BlockSpec(memory_space=pltpu.SMEM)],
        out_specs=[vmem] * 2,
        out_shape=[like((levels, 8, LANES), F32)] * 2,
        compiler_params=params(),
        name="table",
    )(level_table)

    peaks = grouped(peaks, ("dp", "fsdp"), plane)
    peaks = jnp.broadcast_to(jnp.max(peaks, axis=0, keepdims=True), (depth, LANES))
    peaks = grouped(peaks, "dp", line)

    codes, full, scale, factor = pl.pallas_call(
        functools.partial(quantize_kernel, replicas),
        in_specs=[vmem] * 4,
        out_specs=[vmem] * 4,
        out_shape=[
            like((rows, width), BF16),
            like((rows, width), F32),
            like((8, LANES), F32),
            like((1, width), F32),
        ],
        compiler_params=params(),
        name="quantize",
    )(peaks, rotated, centred, lift)

    block = 96
    tile = pl.BlockSpec((block, width), lambda i: (i, 0))
    new_residual = pl.pallas_call(
        residual_kernel,
        grid=(rows // block,),
        in_specs=[tile, tile, pl.BlockSpec((8, LANES), lambda i: (0, 0))],
        out_specs=tile,
        out_shape=like((rows, width), F32),
        compiler_params=params(),
        cost_estimate=pl.CostEstimate(flops=2 * rows * width, bytes_accessed=12 * rows * width, transcendentals=0),
        name="residual",
    )(rotated, full, scale)

    first, second = len(near[0]), len(far[0])
    share = rows // first
    codes = grouped(codes.reshape(first, share, width), "dp", near)
    partial = pl.pallas_call(
        partial_kernel,
        out_shape=like((second, share, width // second), F32),
        compiler_params=params(),
        name="partial",
    )(codes, matrix)
    partial = grouped(partial.astype(F16), "dp", far)
    mean = jnp.sum(partial.astype(F32), axis=0) * 0.125
    mean = jnp.broadcast_to(mean.astype(F16)[None], partial.shape)
    mean = grouped(mean, "dp", far)
    mean = mean.transpose(1, 0, 2).reshape(share, width)
    mean = grouped(jnp.broadcast_to(mean[None], (first, share, width)), "dp", near)
    mean = mean.reshape(rows, width).astype(F32) * factor * sign_flips.astype(F32)
    return mean, new_residual[None]


def solution(mesh):
    placed = (P("dp", "fsdp", None), P("dp", "fsdp", None), P("fsdp", None), P())
    return jax.shard_map(
        on_device,
        mesh=mesh,
        in_specs=placed,
        out_specs=(P("fsdp", None), P("dp", "fsdp", None)),
        check_vma=False,
    )
```

```python
import functools
import math

import jax
import jax.numpy as jnp
from jax import lax
from jax.experimental import pallas as pl
from jax.experimental.pallas import tpu as pltpu
from jax.sharding import PartitionSpec as P

F32, BF16, F16 = jnp.float32, jnp.bfloat16, jnp.float16
FOLD = 256
LANES = 128
VMEM_BYTES = 32 * 1024 * 1024
ROTATE_BYTES = 52 * 1024 * 1024
LOG2E = math.log2(math.e)


def hadamard(width):
    row = lax.broadcasted_iota(jnp.int32, (width, width), 0)
    col = lax.broadcasted_iota(jnp.int32, (width, width), 1)
    common = row & col
    step = 1
    while step < width.bit_length():
        common = common ^ (common >> step)
        step *= 2
    return (1 - 2 * (common & 1)).astype(F32).astype(BF16)


def turn(values, matrix, scale):
    count = values.shape[1] // FOLD
    parts = [values[:, k * FOLD : (k + 1) * FOLD] for k in range(count)]
    step = 1
    while step < count:
        nxt = list(parts)
        for k in range(count):
            if not k & step:
                nxt[k] = parts[k] + parts[k + step]
                nxt[k + step] = parts[k] - parts[k + step]
        parts = nxt
        step *= 2
    turned = []
    for part in parts:
        part = part * scale
        high = part.astype(BF16)
        rest = part - high.astype(F32)
        middle = rest.astype(BF16)
        low = (rest - middle.astype(F32)).astype(BF16)
        dot = functools.partial(jnp.dot, preferred_element_type=F32)
        turned.append(dot(high, matrix) + (dot(middle, matrix) + dot(low, matrix)))
    return turned


def rotate_kernel(
    depth, grad_hbm, flip_hbm, resid_hbm, own_ref, next_ref, across_ref, last_ref, peak_ref, matrix_ref,
    grad, flip, resid, sems,
):
    outs = (own_ref, next_ref, across_ref, last_ref)
    ys = len(outs)
    deep, width = own_ref.shape
    here = lax.div(lax.axis_index("dp"), depth)
    order = (1, 2, 3, 0)
    copies = {}
    for k in order:
        chunk = lax.rem(here + k, ys)
        source, target = pl.ds(pl.multiple_of(chunk * deep, 8), deep), pl.ds(k * deep, deep)
        copies[k] = [
            pltpu.make_async_copy(src.at[source], dst.at[target], sems.at[k, i])
            for i, (src, dst) in enumerate(((grad_hbm, grad), (flip_hbm, flip), (resid_hbm, resid)))
        ]
        for copy in copies[k]:
            copy.start()
    matrix_ref[...] = hadamard(FOLD)

    top = jnp.zeros((8, LANES), F32)
    for k in order:
        for copy in copies[k]:
            copy.wait()
        at = slice(k * deep, (k + 1) * deep)
        signed = grad[at, :] * flip[at, :].astype(F32)
        for j, part in enumerate(turn(signed, matrix_ref[...], 1.0 / math.sqrt(width))):
            cols = slice(j * FOLD, (j + 1) * FOLD)
            rotated = part + resid[at, cols]
            outs[k][:, cols] = rotated
            size = jnp.abs(rotated)
            for lane in range(0, FOLD, LANES):
                tiles = size[:, lane : lane + LANES].reshape(-1, 8, LANES)
                top = jnp.maximum(top, jnp.max(tiles, axis=0))
    peak_ref[...] = jnp.broadcast_to(jnp.max(top, axis=0, keepdims=True), peak_ref.shape)


def table_kernel(level_ref, centre_ref, lift_ref):
    count = level_ref.shape[0]
    bottom = level_ref[0].astype(F32)
    upper = level_ref[count - 1].astype(F32)
    middle = (bottom + upper) * 0.5
    for k in range(count):
        centred = jnp.full((8, LANES), level_ref[k].astype(F32) - middle, F32)
        centre_ref[k] = centred
        lift_ref[k] = centred * centred * (-LOG2E / 72.0)


def soft_codes(rows, cols, load, reach, centre_ref, lift_ref):
    place = [load(r, l) * reach for l in cols for r in rows]
    numer, denom = [None] * len(place), [None] * len(place)
    for k in range(centre_ref.shape[0]):
        centred, lift = centre_ref[k], lift_ref[k]
        for i in range(len(place)):
            weight = jnp.exp2(place[i] * centred + lift)
            moment = weight * centred
            numer[i] = moment if k == 0 else numer[i] + moment
            denom[i] = weight if k == 0 else denom[i] + weight
    return [n / d for n, d in zip(numer, denom)]


def scales(peaks_ref, centre_ref):
    top = jnp.max(peaks_ref[...], axis=0, keepdims=True)
    peak = jnp.max(top, axis=1, keepdims=True) + 1e-06
    peak = jnp.broadcast_to(peak, (8, LANES))
    half_span = (centre_ref[centre_ref.shape[0] - 1] - centre_ref[0]) * 0.5
    return peak / half_span, half_span / peak * (LOG2E / 36.0)


def partial_kernel(
    replicas, peaks_ref, p0, p1, p2, p3, centre_ref, lift_ref, matrix_ref, out_ref, factor_ref, total_ref
):
    scale, reach = scales(peaks_ref, centre_ref)
    pieces = (p0, p1, p2, p3)
    rows, width = p0.shape
    factor_ref[...] = jnp.tile(scale[0:1] * (8.0 / replicas), (1, width // LANES))
    wide = 4 * LANES
    per_row = width // wide

    def chunk(step, carry):
        row = pl.multiple_of((step // per_row) * 8, 8)
        col = pl.multiple_of((step % per_row) * wide, wide)

        def at(l):
            return pl.ds(row, 8), pl.ds(col + l * LANES, LANES)

        codes = soft_codes(pieces, range(4), lambda piece, l: piece[at(l)], reach, centre_ref, lift_ref)
        for l in range(4):
            total = None
            for code in codes[l * 4 : (l + 1) * 4]:
                code = code.astype(BF16).astype(F32)
                total = code if total is None else total + code
            total_ref[at(l)] = total
        return carry

    lax.fori_loop(0, (rows // 8) * per_row, chunk, 0, unroll=2)
    turned = turn(total_ref[...], matrix_ref[...], 1.0 / math.sqrt(width))
    half = rows // 2
    for k, part in enumerate(turned):
        for at in range(0, FOLD, LANES):
            for low in range(2):
                piece = (k * FOLD + at) // LANES * 2 + low
                out_ref[piece] = part[low * half : (low + 1) * half, at : at + LANES]


def residual_kernel(depth, peaks_ref, r0, r1, r2, r3, centre_ref, lift_ref, out_hbm, out, sems):
    scale, reach = scales(peaks_ref, centre_ref)
    deep, width = r0.shape
    here = lax.div(lax.axis_index("dp"), depth)
    copies = []
    for c, rot_ref in enumerate((r0, r1, r2, r3)):

        def chunk(step, carry, c=c, rot_ref=rot_ref):
            row = pl.multiple_of(step * 16, 16)

            def at(r, l):
                return pl.ds(row + 8 * r, 8), slice(l * LANES, (l + 1) * LANES)

            tiles = [(r, l) for l in range(width // LANES) for r in range(2)]
            codes = soft_codes(
                range(2), range(width // LANES), lambda r, l: rot_ref[at(r, l)], reach, centre_ref, lift_ref
            )
            for (r, l), code in zip(tiles, codes):
                out[(c,) + at(r, l)] = rot_ref[at(r, l)] - code * scale
            return carry

        lax.fori_loop(0, deep // 16, chunk, 0, unroll=2)
        target = pl.ds(pl.multiple_of(lax.rem(here + c, 4) * deep, 8), deep)
        copies.append(pltpu.make_async_copy(out.at[c], out_hbm.at[target], sems.at[c]))
        copies[c].start()
    for copy in copies:
        copy.wait()


def grouped(pieces, axes, groups):
    return lax.all_to_all(pieces, axes, 0, 0, axis_index_groups=groups)


def on_device(gradient, residual, sign_flips, level_table):
    _, rows, width = gradient.shape
    levels = level_table.shape[0]
    replicas, splits = lax.axis_size("dp"), lax.axis_size("fsdp")
    depth = 16
    ys, pairs = range(replicas // depth), range(depth // 2)
    near = [[y * depth + 2 * h + l for y in ys for l in range(2)] for h in pairs]
    far = [[y * depth + 2 * h + l for h in pairs] for y in ys for l in range(2)]
    line = [[y * depth + z for z in range(depth)] for y in ys]
    plane = [[(y * depth + z) * splits + f for y in ys for f in range(splits)] for z in range(depth)]
    params = functools.partial(pltpu.CompilerParams, vmem_limit_bytes=VMEM_BYTES)
    hbm, vmem = pl.BlockSpec(memory_space=pltpu.HBM), pl.BlockSpec(memory_space=pltpu.VMEM)
    like = jax.ShapeDtypeStruct

    count = len(ys)
    deep = rows // count
    *chunks, peaks, matrix = pl.pallas_call(
        functools.partial(rotate_kernel, depth),
        in_specs=[hbm] * 3,
        out_specs=[vmem] * (count + 2),
        out_shape=[like((deep, width), F32)] * count
        + [like((len(plane[0]), LANES), F32), like((FOLD, FOLD), BF16)],
        scratch_shapes=[
            pltpu.VMEM((rows, width), F32),
            pltpu.VMEM((rows, width), jnp.int32),
            pltpu.VMEM((rows, width), F32),
            pltpu.SemaphoreType.DMA((count, 3)),
        ],
        compiler_params=pltpu.CompilerParams(vmem_limit_bytes=ROTATE_BYTES),
        name="rotate",
    )(gradient[0], sign_flips, residual[0])

    def ahead(chunk, k):
        hops = [(y * depth + z, (y + k) % count * depth + z) for y in ys for z in range(depth)]
        return lax.ppermute(chunk, "dp", hops)

    pieces = [chunks[0]] + [ahead(chunks[k], k) for k in range(1, count)]
    centred, lift = pl.pallas_call(
        table_kernel,
        in_specs=[pl.BlockSpec(memory_space=pltpu.SMEM)],
        out_specs=[vmem] * 2,
        out_shape=[like((levels, 8, LANES), F32)] * 2,
        compiler_params=params(),
        name="table",
    )(level_table)

    peaks = grouped(peaks, ("dp", "fsdp"), plane)
    peaks = jnp.broadcast_to(jnp.max(peaks, axis=0, keepdims=True), (depth, LANES))
    peaks = grouped(peaks, "dp", line)

    first, second = len(near[0]), len(far[0])
    share = rows // first
    partial, factor = pl.pallas_call(
        functools.partial(partial_kernel, replicas),
        in_specs=[vmem] * 8,
        out_specs=[vmem] * 2,
        out_shape=[like((depth, share, width // second), F32), like((1, width), F32)],
        scratch_shapes=[pltpu.VMEM((deep, width), F32)],
        compiler_params=params(),
        name="partial",
    )(peaks, *pieces, centred, lift, matrix)
    new_residual = pl.pallas_call(
        functools.partial(residual_kernel, depth),
        in_specs=[vmem] * 7,
        out_specs=hbm,
        out_shape=like((rows, width), F32),
        scratch_shapes=[pltpu.VMEM((count, deep, width), F32), pltpu.SemaphoreType.DMA((count,))],
        compiler_params=params(),
        cost_estimate=pl.CostEstimate(flops=100 * rows * width, bytes_accessed=12 * rows * width, transcendentals=16 * rows * width),
        name="residual",
    )(peaks, *chunks, centred, lift)

    partial = grouped(partial.astype(F16), "dp", line)
    partial, new_residual = lax.optimization_barrier((partial, new_residual))
    mean = jnp.sum(partial.astype(F32), axis=0) * 0.125
    mean = jnp.broadcast_to(mean.astype(F16)[None], (second,) + mean.shape)
    mean = grouped(mean, "dp", far)
    mean = mean.transpose(1, 0, 2).reshape(share, width)
    mean = grouped(jnp.broadcast_to(mean[None], (first, share, width)), "dp", near)
    mean = mean.reshape(rows, width).astype(F32) * factor * sign_flips.astype(F32)
    return mean, new_residual[None]


def solution(mesh):
    placed = (P("dp", "fsdp", None), P("dp", "fsdp", None), P("fsdp", None), P())
    return jax.shard_map(
        on_device,
        mesh=mesh,
        in_specs=placed,
        out_specs=(P("fsdp", None), P("dp", "fsdp", None)),
        check_vma=False,
    )
```

```python
import functools
import math

import jax
import jax.numpy as jnp
from jax import lax
from jax.experimental import pallas as pl
from jax.experimental.pallas import tpu as pltpu
from jax.sharding import PartitionSpec as P

F32, BF16, F16 = jnp.float32, jnp.bfloat16, jnp.float16
FOLD = 256
LANES = 128
VMEM_BYTES = 32 * 1024 * 1024
ROTATE_BYTES = 52 * 1024 * 1024
LOG2E = math.log2(math.e)


def hadamard(width):
    row = lax.broadcasted_iota(jnp.int32, (width, width), 0)
    col = lax.broadcasted_iota(jnp.int32, (width, width), 1)
    common = row & col
    step = 1
    while step < width.bit_length():
        common = common ^ (common >> step)
        step *= 2
    return (1 - 2 * (common & 1)).astype(F32).astype(BF16)


def turn(values, matrix, scale):
    count = values.shape[1] // FOLD
    parts = [values[:, k * FOLD : (k + 1) * FOLD] for k in range(count)]
    step = 1
    while step < count:
        nxt = list(parts)
        for k in range(count):
            if not k & step:
                nxt[k] = parts[k] + parts[k + step]
                nxt[k + step] = parts[k] - parts[k + step]
        parts = nxt
        step *= 2
    turned = []
    for part in parts:
        part = part * scale
        high = part.astype(BF16)
        rest = part - high.astype(F32)
        middle = rest.astype(BF16)
        low = (rest - middle.astype(F32)).astype(BF16)
        dot = functools.partial(jnp.dot, preferred_element_type=F32)
        turned.append(dot(high, matrix) + (dot(middle, matrix) + dot(low, matrix)))
    return turned


def rotate_kernel(
    grad_hbm, flip_hbm, resid_hbm, rot_ref, peak_ref, matrix_ref,
    grad, flip, resid, sems,
):
    rows, width = rot_ref.shape
    chunks = sems.shape[0]
    deep = rows // chunks
    copies = []
    for c in range(chunks):
        at = pl.ds(c * deep, deep)
        copies.append([])
        for k, (src, dst) in enumerate(((grad_hbm, grad), (flip_hbm, flip), (resid_hbm, resid))):
            copies[c].append(pltpu.make_async_copy(src.at[at], dst.at[at], sems.at[c, k]))
            copies[c][k].start()

    matrix_ref[...] = hadamard(FOLD)

    top = jnp.zeros((8, LANES), F32)
    for c in range(chunks):
        for copy in copies[c]:
            copy.wait()
        at = slice(c * deep, (c + 1) * deep)
        signed = grad[at, :] * flip[at, :].astype(F32)
        for k, part in enumerate(turn(signed, matrix_ref[...], 1.0 / math.sqrt(width))):
            cols = slice(k * FOLD, (k + 1) * FOLD)
            rotated = part + resid[at, cols]
            rot_ref[at, cols] = rotated
            size = jnp.abs(rotated)
            for lane in range(0, FOLD, LANES):
                tiles = size[:, lane : lane + LANES].reshape(-1, 8, LANES)
                top = jnp.maximum(top, jnp.max(tiles, axis=0))
    peak_ref[...] = jnp.broadcast_to(jnp.max(top, axis=0, keepdims=True), peak_ref.shape)


def table_kernel(level_ref, centre_ref, lift_ref):
    count = level_ref.shape[0]
    bottom = level_ref[0].astype(F32)
    upper = level_ref[count - 1].astype(F32)
    middle = (bottom + upper) * 0.5
    for k in range(count):
        centred = jnp.full((8, LANES), level_ref[k].astype(F32) - middle, F32)
        centre_ref[k] = centred
        lift_ref[k] = centred * centred * (-LOG2E / 72.0)


def quantize_kernel(replicas, peaks_ref, rot_ref, centre_ref, lift_ref, code_ref, full_ref, scale_ref, factor_ref):
    count = centre_ref.shape[0]
    rows, width = rot_ref.shape
    top = jnp.max(peaks_ref[...], axis=0, keepdims=True)
    peak = jnp.max(top, axis=1, keepdims=True) + 1e-06
    peak = jnp.broadcast_to(peak, (8, LANES))
    half_span = (centre_ref[count - 1] - centre_ref[0]) * 0.5
    scale = peak / half_span
    scale_ref[...] = scale
    factor_ref[...] = jnp.tile(scale[0:1] * (8.0 / replicas), (1, width // LANES))
    reach = half_span / peak * (LOG2E / 36.0)
    groups = [(r, slice(l * LANES, (l + 1) * LANES)) for l in range(width // LANES) for r in range(2)]

    def chunk(step, carry):
        row = pl.multiple_of(step * 16, 16)
        place = [rot_ref[pl.ds(row + 8 * r, 8), l] * reach for r, l in groups]
        numer, denom = [None] * len(groups), [None] * len(groups)
        for k in range(count):
            centred, lift = centre_ref[k], lift_ref[k]
            for i in range(len(groups)):
                weight = jnp.exp2(place[i] * centred + lift)
                moment = weight * centred
                numer[i] = moment if k == 0 else numer[i] + moment
                denom[i] = weight if k == 0 else denom[i] + weight
        for i in range(0, len(groups), 2):
            code = jnp.concatenate([numer[i] / denom[i], numer[i + 1] / denom[i + 1]], axis=0)
            full_ref[pl.ds(row, 16), groups[i][1]] = code
            code_ref[pl.ds(row, 16), groups[i][1]] = code.astype(BF16)
        return carry

    lax.fori_loop(0, rows // 16, chunk, 0, unroll=2)


def residual_kernel(rot_ref, full_ref, scale_ref, out_ref):
    scale = scale_ref[0:1, 0:1]
    out_ref[...] = rot_ref[...] - full_ref[...] * scale


def partial_kernel(codes_ref, matrix_ref, out_ref):
    width = codes_ref.shape[2]
    total = codes_ref[0].astype(F32)
    for k in range(1, codes_ref.shape[0]):
        total = total + codes_ref[k].astype(F32)
    turned = turn(total, matrix_ref[...], 1.0 / math.sqrt(width))
    for k, part in enumerate(turned):
        for at in range(0, FOLD, LANES):
            out_ref[(k * FOLD + at) // LANES] = part[:, at : at + LANES]


def grouped(pieces, axes, groups):
    return lax.all_to_all(pieces, axes, 0, 0, axis_index_groups=groups)


def on_device(gradient, residual, sign_flips, level_table):
    _, rows, width = gradient.shape
    levels = level_table.shape[0]
    replicas, splits = lax.axis_size("dp"), lax.axis_size("fsdp")
    depth = 16
    ys, pairs = range(replicas // depth), range(depth // 2)
    zs = [(depth // 2 + z) % depth for z in range(depth)]
    near = [[y * depth + 2 * h + l for y in ys for l in range(2)] for h in pairs]
    far = [[y * depth + z for z in zs[l::2]] for y in ys for l in range(2)]
    line = [[y * depth + z for z in zs] for y in ys]
    plane = [
        [(y * depth + z) * splits + f for y in reversed(ys) for f in range(splits - 2, -1, -1)]
        + [(y * depth + z) * splits + splits - 1 for y in ys]
        for z in range(depth)
    ]
    params = functools.partial(pltpu.CompilerParams, vmem_limit_bytes=VMEM_BYTES)
    hbm, vmem = pl.BlockSpec(memory_space=pltpu.HBM), pl.BlockSpec(memory_space=pltpu.VMEM)
    like = jax.ShapeDtypeStruct

    chunks = 4
    rotated, peaks, matrix = pl.pallas_call(
        rotate_kernel,
        in_specs=[hbm] * 3,
        out_specs=[vmem] * 3,
        out_shape=[
            like((rows, width), F32),
            like((len(plane[0]), LANES), F32),
            like((FOLD, FOLD), BF16),
        ],
        scratch_shapes=[
            pltpu.VMEM((rows, width), F32),
            pltpu.VMEM((rows, width), jnp.int32),
            pltpu.VMEM((rows, width), F32),
            pltpu.SemaphoreType.DMA((chunks, 3)),
        ],
        compiler_params=pltpu.CompilerParams(vmem_limit_bytes=ROTATE_BYTES),
        name="rotate",
    )(gradient[0], sign_flips, residual[0])
    centred, lift = pl.pallas_call(
        table_kernel,
        in_specs=[pl.BlockSpec(memory_space=pltpu.SMEM)],
        out_specs=[vmem] * 2,
        out_shape=[like((levels, 8, LANES), F32)] * 2,
        compiler_params=params(),
        name="table",
    )(level_table)

    peaks = grouped(peaks, ("dp", "fsdp"), plane)
    peaks = jnp.broadcast_to(jnp.max(peaks, axis=0, keepdims=True), (depth, LANES))
    peaks = grouped(peaks, "dp", line)

    codes, full, scale, factor = pl.pallas_call(
        functools.partial(quantize_kernel, replicas),
        in_specs=[vmem] * 4,
        out_specs=[vmem] * 4,
        out_shape=[
            like((rows, width), BF16),
            like((rows, width), F32),
            like((8, LANES), F32),
            like((1, width), F32),
        ],
        compiler_params=params(),
        name="quantize",
    )(peaks, rotated, centred, lift)

    block = 96
    tile = pl.BlockSpec((block, width), lambda i: (i, 0))
    new_residual = pl.pallas_call(
        residual_kernel,
        grid=(rows // block,),
        in_specs=[tile, tile, pl.BlockSpec((8, LANES), lambda i: (0, 0))],
        out_specs=tile,
        out_shape=like((rows, width), F32),
        compiler_params=params(),
        cost_estimate=pl.CostEstimate(flops=2 * rows * width, bytes_accessed=12 * rows * width, transcendentals=0),
        name="residual",
    )(rotated, full, scale)

    first, second = len(near[0]), len(far[0])
    share = rows // first
    codes = grouped(codes.reshape(first, share, width), "dp", near)
    partial = pl.pallas_call(
        partial_kernel,
        out_shape=like((second, share, width // second), F32),
        compiler_params=params(),
        name="partial",
    )(codes, matrix)
    partial = grouped(partial.astype(F16), "dp", far)
    partial, new_residual = lax.optimization_barrier((partial, new_residual))
    mean = jnp.sum(partial.astype(F32), axis=0) * 0.125
    mean = jnp.broadcast_to(mean.astype(F16)[None], partial.shape)
    mean = grouped(mean, "dp", far)
    mean = mean.transpose(1, 0, 2).reshape(share, width)
    mean = grouped(jnp.broadcast_to(mean[None], (first, share, width)), "dp", near)
    mean = mean.reshape(rows, width).astype(F32) * factor * sign_flips.astype(F32)
    return mean, new_residual[None]


def solution(mesh):
    placed = (P("dp", "fsdp", None), P("dp", "fsdp", None), P("fsdp", None), P())
    return jax.shard_map(
        on_device,
        mesh=mesh,
        in_specs=placed,
        out_specs=(P("fsdp", None), P("dp", "fsdp", None)),
        check_vma=False,
    )
```

```python
import functools
import math

import jax
import jax.numpy as jnp
from jax import lax
from jax.experimental import pallas as pl
from jax.experimental.pallas import tpu as pltpu
from jax.sharding import PartitionSpec as P

F32, BF16, F16 = jnp.float32, jnp.bfloat16, jnp.float16
FOLD = 256
LANES = 128
VMEM_BYTES = 32 * 1024 * 1024
ROTATE_BYTES = 52 * 1024 * 1024
LOG2E = math.log2(math.e)


def hadamard(width):
    row = lax.broadcasted_iota(jnp.int32, (width, width), 0)
    col = lax.broadcasted_iota(jnp.int32, (width, width), 1)
    common = row & col
    step = 1
    while step < width.bit_length():
        common = common ^ (common >> step)
        step *= 2
    return (1 - 2 * (common & 1)).astype(F32).astype(BF16)


def butterflies(values):
    count = values.shape[1] // FOLD
    parts = [values[:, k * FOLD : (k + 1) * FOLD] for k in range(count)]
    step = 1
    while step < count:
        nxt = list(parts)
        for k in range(count):
            if not k & step:
                nxt[k] = parts[k] + parts[k + step]
                nxt[k + step] = parts[k] - parts[k + step]
        parts = nxt
        step *= 2
    return parts


def turn(part, matrix):
    high = part.astype(BF16)
    rest = part - high.astype(F32)
    middle = rest.astype(BF16)
    low = (rest - middle.astype(F32)).astype(BF16)
    dot = functools.partial(jnp.dot, preferred_element_type=F32)
    return dot(high, matrix) + (dot(middle, matrix) + dot(low, matrix))


def rotate_kernel(
    grad_hbm, flip_hbm, resid_hbm, rot_ref, peak_ref, matrix_ref,
    grad, flip, resid, sems,
):
    rows, width = rot_ref.shape
    chunks = sems.shape[0]
    deep = rows // chunks
    copies = []
    for c in range(chunks):
        at = pl.ds(c * deep, deep)
        copies.append([])
        for k, (src, dst) in enumerate(((grad_hbm, grad), (flip_hbm, flip), (resid_hbm, resid))):
            copies[c].append(pltpu.make_async_copy(src.at[at], dst.at[at], sems.at[c, k]))
            copies[c][k].start()

    matrix_ref[...] = hadamard(FOLD)

    top = jnp.zeros((8, LANES), F32)
    for c in range(chunks):
        for copy in copies[c]:
            copy.wait()
        at = slice(c * deep, (c + 1) * deep)
        signed = grad[at, :] * flip[at, :].astype(F32)
        for k, part in enumerate(butterflies(signed * (1.0 / math.sqrt(width)))):
            cols = slice(k * FOLD, (k + 1) * FOLD)
            rotated = turn(part, matrix_ref[...]) + resid[at, cols]
            rot_ref[at, cols] = rotated
            size = jnp.abs(rotated)
            for lane in range(0, FOLD, LANES):
                tiles = size[:, lane : lane + LANES].reshape(-1, 8, LANES)
                top = jnp.maximum(top, jnp.max(tiles, axis=0))
    peak_ref[...] = jnp.broadcast_to(jnp.max(top, axis=0, keepdims=True), peak_ref.shape)


def quantize_kernel(
    replicas, peaks_ref, rot_ref, level_ref, code_ref, full_ref, scale_ref, factor_ref, centre_ref, lift_ref
):
    count = level_ref.shape[1]
    levels = level_ref[...].astype(F32)
    bottom, upper = levels[:, 0:1], levels[:, count - 1 : count]
    centred = levels - (bottom + upper) * 0.5
    lift = centred * centred * (-LOG2E / 72.0)
    for k in range(count):
        centre_ref[k] = jnp.broadcast_to(centred[:, k : k + 1], (8, LANES))
        lift_ref[k] = jnp.broadcast_to(lift[:, k : k + 1], (8, LANES))
    rows, width = rot_ref.shape
    top = jnp.max(peaks_ref[...], axis=0, keepdims=True)
    peak = jnp.max(top, axis=1, keepdims=True) + 1e-06
    peak = jnp.broadcast_to(peak, (8, LANES))
    half_span = (centre_ref[count - 1] - centre_ref[0]) * 0.5
    scale = peak / half_span
    scale_ref[...] = scale
    factor_ref[...] = jnp.tile(scale[0:1] * (8.0 / replicas), (1, width // LANES))
    reach = half_span / peak * (LOG2E / 36.0)
    groups = [(r, slice(l * LANES, (l + 1) * LANES)) for l in range(width // LANES) for r in range(2)]

    def chunk(step, carry):
        row = pl.multiple_of(step * 16, 16)
        place = [rot_ref[pl.ds(row + 8 * r, 8), l] * reach for r, l in groups]
        numer, denom = [None] * len(groups), [None] * len(groups)
        for k in range(count):
            centred, lift = centre_ref[k], lift_ref[k]
            for i in range(len(groups)):
                weight = jnp.exp2(place[i] * centred + lift)
                moment = weight * centred
                numer[i] = moment if k == 0 else numer[i] + moment
                denom[i] = weight if k == 0 else denom[i] + weight
        for i in range(0, len(groups), 2):
            code = jnp.concatenate([numer[i] / denom[i], numer[i + 1] / denom[i + 1]], axis=0)
            full_ref[pl.ds(row, 16), groups[i][1]] = code
            code_ref[pl.ds(row, 16), groups[i][1]] = code.astype(BF16)
        return carry

    lax.fori_loop(0, rows // 16, chunk, 0, unroll=2)


def residual_kernel(rot_ref, full_ref, scale_ref, out_ref):
    scale = scale_ref[0:1, 0:1]
    out_ref[...] = rot_ref[...] - full_ref[...] * scale


def partial_kernel(codes_ref, matrix_ref, out_ref):
    width = codes_ref.shape[2]
    total = codes_ref[0].astype(F32)
    for k in range(1, codes_ref.shape[0]):
        total = total + codes_ref[k].astype(F32)
    parts = butterflies(total * (1.0 / math.sqrt(width)))
    turned = turn(jnp.concatenate(parts, axis=0), matrix_ref[...])
    for k, part in enumerate(jnp.split(turned, len(parts), axis=0)):
        for at in range(0, FOLD, LANES):
            out_ref[(k * FOLD + at) // LANES] = part[:, at : at + LANES]


def grouped(pieces, axes, groups):
    return lax.all_to_all(pieces, axes, 0, 0, axis_index_groups=groups)


def on_device(gradient, residual, sign_flips, level_table):
    _, rows, width = gradient.shape
    levels = level_table.shape[0]
    replicas, splits = lax.axis_size("dp"), lax.axis_size("fsdp")
    depth = 16
    ys, pairs = range(replicas // depth), range(depth // 2)
    ring = sorted(range(depth), key=lambda z: (z != depth // 2, -min((z - depth // 2) % depth, (depth // 2 - z) % depth)))
    near = [[y * depth + 2 * h + l for y in reversed(ys) for l in range(2)] for h in pairs]
    far = [[y * depth + z + l for z in ring if z % 2 == 0] for y in ys for l in range(2)]
    line = [[y * depth + z for z in ring] for y in ys]
    plane = [
        [(y * depth + z) * splits + f for y in reversed(ys) for f in range(splits - 2, -1, -1)]
        + [(y * depth + z) * splits + splits - 1 for y in ys]
        for z in range(depth)
    ]
    params = functools.partial(pltpu.CompilerParams, vmem_limit_bytes=VMEM_BYTES)
    hbm, vmem = pl.BlockSpec(memory_space=pltpu.HBM), pl.BlockSpec(memory_space=pltpu.VMEM)
    like = jax.ShapeDtypeStruct

    chunks = 4
    rotated, peaks, matrix = pl.pallas_call(
        rotate_kernel,
        in_specs=[hbm] * 3,
        out_specs=[vmem] * 3,
        out_shape=[
            like((rows, width), F32),
            like((len(plane[0]), LANES), F32),
            like((FOLD, FOLD), BF16),
        ],
        scratch_shapes=[
            pltpu.VMEM((rows, width), F32),
            pltpu.VMEM((rows, width), jnp.int32),
            pltpu.VMEM((rows, width), F32),
            pltpu.SemaphoreType.DMA((chunks, 3)),
        ],
        compiler_params=pltpu.CompilerParams(vmem_limit_bytes=ROTATE_BYTES),
        name="rotate",
    )(gradient[0], sign_flips, residual[0])
    peaks = grouped(peaks, ("dp", "fsdp"), plane)
    peaks = jnp.broadcast_to(jnp.max(peaks, axis=0, keepdims=True), (depth, LANES))
    peaks = grouped(peaks, "dp", line)

    codes, full, scale, factor = pl.pallas_call(
        functools.partial(quantize_kernel, replicas),
        in_specs=[vmem] * 3,
        out_specs=[vmem] * 4,
        out_shape=[
            like((rows, width), BF16),
            like((rows, width), F32),
            like((8, LANES), F32),
            like((1, width), F32),
        ],
        scratch_shapes=[pltpu.VMEM((levels, 8, LANES), F32)] * 2,
        compiler_params=params(),
        name="quantize",
    )(peaks, rotated, level_table.reshape(1, levels))

    block = 96
    tile = pl.BlockSpec((block, width), lambda i: (i, 0))
    new_residual = pl.pallas_call(
        residual_kernel,
        grid=(rows // block,),
        in_specs=[tile, tile, pl.BlockSpec((8, LANES), lambda i: (0, 0))],
        out_specs=tile,
        out_shape=like((rows, width), F32),
        compiler_params=params(),
        cost_estimate=pl.CostEstimate(flops=2 * rows * width, bytes_accessed=12 * rows * width, transcendentals=0),
        name="residual",
    )(rotated, full, scale)

    first, second = len(near[0]), len(far[0])
    share = rows // first
    codes = grouped(codes.reshape(first, share, width), "dp", near)
    partial = pl.pallas_call(
        partial_kernel,
        out_shape=like((second, share, width // second), F32),
        compiler_params=params(),
        name="partial",
    )(codes, matrix)
    partial = grouped(partial.astype(F16), "dp", far)
    partial, new_residual = lax.optimization_barrier((partial, new_residual))
    mean = jnp.sum(partial.astype(F32), axis=0) * 0.125
    mean = jnp.broadcast_to(mean.astype(F16)[None], partial.shape)
    mean = grouped(mean, "dp", far)
    mean = mean.transpose(1, 0, 2).reshape(share, width)
    mean = grouped(jnp.broadcast_to(mean[None], (first, share, width)), "dp", near)
    mean = mean.reshape(rows, width).astype(F32) * factor * sign_flips.astype(F32)
    return mean, new_residual[None]


def solution(mesh):
    placed = (P("dp", "fsdp", None), P("dp", "fsdp", None), P("fsdp", None), P())
    return jax.shard_map(
        on_device,
        mesh=mesh,
        in_specs=placed,
        out_specs=(P("fsdp", None), P("dp", "fsdp", None)),
        check_vma=False,
    )
```

```python
import functools
import math

import jax
import jax.numpy as jnp
from jax import lax
from jax.experimental import pallas as pl
from jax.experimental.pallas import tpu as pltpu
from jax.sharding import PartitionSpec as P

F32, BF16, F16 = jnp.float32, jnp.bfloat16, jnp.float16
FOLD = 256
LANES = 128
VMEM_BYTES = 32 * 1024 * 1024
ROTATE_BYTES = 52 * 1024 * 1024
LOG2E = math.log2(math.e)


def hadamard(width):
    row = lax.broadcasted_iota(jnp.int32, (width, width), 0)
    col = lax.broadcasted_iota(jnp.int32, (width, width), 1)
    common = row & col
    step = 1
    while step < width.bit_length():
        common = common ^ (common >> step)
        step *= 2
    return (1 - 2 * (common & 1)).astype(F32).astype(BF16)


def butterflies(values):
    count = values.shape[1] // FOLD
    parts = [values[:, k * FOLD : (k + 1) * FOLD] for k in range(count)]
    step = 1
    while step < count:
        nxt = list(parts)
        for k in range(count):
            if not k & step:
                nxt[k] = parts[k] + parts[k + step]
                nxt[k + step] = parts[k] - parts[k + step]
        parts = nxt
        step *= 2
    return parts


def turn(part, matrix):
    high = part.astype(BF16)
    rest = part - high.astype(F32)
    middle = rest.astype(BF16)
    low = (rest - middle.astype(F32)).astype(BF16)
    dot = functools.partial(jnp.dot, preferred_element_type=F32)
    return dot(high, matrix) + (dot(middle, matrix) + dot(low, matrix))


def rotate_kernel(
    grad_hbm, flip_hbm, resid_hbm, rot_ref, peak_ref, matrix_ref,
    grad, flip, resid, sems,
):
    rows, width = rot_ref.shape
    chunks = sems.shape[0]
    deep = rows // chunks
    copies = []
    for c in range(chunks):
        at = pl.ds(c * deep, deep)
        copies.append([])
        for k, (src, dst) in enumerate(((grad_hbm, grad), (flip_hbm, flip), (resid_hbm, resid))):
            copies[c].append(pltpu.make_async_copy(src.at[at], dst.at[at], sems.at[c, k]))
            copies[c][k].start()

    matrix_ref[...] = hadamard(FOLD)

    top = jnp.zeros((8, LANES), F32)
    for c in range(chunks):
        for copy in copies[c]:
            copy.wait()
        at = slice(c * deep, (c + 1) * deep)
        signed = grad[at, :] * flip[at, :].astype(F32)
        for k, part in enumerate(butterflies(signed * (1.0 / math.sqrt(width)))):
            cols = slice(k * FOLD, (k + 1) * FOLD)
            rotated = turn(part, matrix_ref[...]) + resid[at, cols]
            rot_ref[at, cols] = rotated
            size = jnp.abs(rotated)
            for lane in range(0, FOLD, LANES):
                tiles = size[:, lane : lane + LANES].reshape(-1, 8, LANES)
                top = jnp.maximum(top, jnp.max(tiles, axis=0))
    peak_ref[...] = jnp.broadcast_to(jnp.max(top, axis=0, keepdims=True), peak_ref.shape)


def quantize_kernel(
    replicas, peaks_ref, rot_ref, level_ref, code_ref, full_ref, scale_ref, factor_ref, centre_ref, lift_ref
):
    count = level_ref.shape[1]
    levels = level_ref[...].astype(F32)
    bottom, upper = levels[:, 0:1], levels[:, count - 1 : count]
    centred = levels - (bottom + upper) * 0.5
    lift = centred * centred * (-LOG2E / 72.0)
    for k in range(count):
        centre_ref[k] = jnp.broadcast_to(centred[:, k : k + 1], (8, LANES))
        lift_ref[k] = jnp.broadcast_to(lift[:, k : k + 1], (8, LANES))
    rows, width = rot_ref.shape
    top = jnp.max(peaks_ref[...], axis=0, keepdims=True)
    peak = jnp.max(top, axis=1, keepdims=True) + 1e-06
    peak = jnp.broadcast_to(peak, (8, LANES))
    half_span = (centre_ref[count - 1] - centre_ref[0]) * 0.5
    scale = peak / half_span
    scale_ref[...] = scale
    factor_ref[...] = jnp.tile(scale[0:1] * (8.0 / replicas), (1, width // LANES))
    reach = half_span / peak * (LOG2E / 36.0)
    groups = [(r, slice(l * LANES, (l + 1) * LANES)) for l in range(width // LANES) for r in range(2)]

    def chunk(step, carry):
        row = pl.multiple_of(step * 16, 16)
        place = [rot_ref[pl.ds(row + 8 * r, 8), l] * reach for r, l in groups]
        numer, denom = [None] * len(groups), [None] * len(groups)
        for k in range(count):
            centred, lift = centre_ref[k], lift_ref[k]
            for i in range(len(groups)):
                weight = jnp.exp2(place[i] * centred + lift)
                moment = weight * centred
                numer[i] = moment if k == 0 else numer[i] + moment
                denom[i] = weight if k == 0 else denom[i] + weight
        for i in range(0, len(groups), 2):
            code = jnp.concatenate([numer[i] / denom[i], numer[i + 1] / denom[i + 1]], axis=0)
            full_ref[pl.ds(row, 16), groups[i][1]] = code
            code_ref[pl.ds(row, 16), groups[i][1]] = code.astype(BF16)
        return carry

    lax.fori_loop(0, rows // 16, chunk, 0, unroll=2)


def residual_kernel(rot_ref, full_ref, scale_ref, out_ref):
    scale = scale_ref[0:1, 0:1]
    out_ref[...] = rot_ref[...] - full_ref[...] * scale


def partial_kernel(chunk_of, codes_ref, matrix_ref, out_ref):
    width = codes_ref.shape[2]
    total = codes_ref[0].astype(F32)
    for k in range(1, codes_ref.shape[0]):
        total = total + codes_ref[k].astype(F32)
    parts = butterflies(total * (1.0 / math.sqrt(width)))
    turned = turn(jnp.concatenate(parts, axis=0), matrix_ref[...])
    chunks = jnp.split(turned, len(parts), axis=0)
    for i, chunk in enumerate(chunk_of):
        out_ref[i] = chunks[chunk]


def grouped(pieces, axes, groups):
    return lax.all_to_all(pieces, axes, 0, 0, axis_index_groups=groups)


def on_device(gradient, residual, sign_flips, level_table):
    _, rows, width = gradient.shape
    levels = level_table.shape[0]
    replicas, splits = lax.axis_size("dp"), lax.axis_size("fsdp")
    depth = 16
    ys, pairs = range(replicas // depth), range(depth // 2)
    ring = sorted(range(depth), key=lambda z: (z != depth // 2, -min((z - depth // 2) % depth, (depth // 2 - z) % depth)))
    near = [[y * depth + 2 * h + l for y in reversed(ys) for l in range(2)] for h in pairs]
    far = [[y * depth + z + l for z in ring if z % 2 == 0] for y in ys for l in range(2)]
    halves = ((8, 4, 10, 6), (14, 2, 12, 0))
    half = [[y * depth + z + l for z in members] for members in halves for y in ys for l in range(2)]
    chunk_of = [members.index(z) for z in ring if z % 2 == 0 for members in halves if z in members]
    line = [[y * depth + z for z in ring] for y in ys]
    plane = [
        [(y * depth + z) * splits + f for y in reversed(ys) for f in range(splits - 2, -1, -1)]
        + [(y * depth + z) * splits + splits - 1 for y in ys]
        for z in range(depth)
    ]
    params = functools.partial(pltpu.CompilerParams, vmem_limit_bytes=VMEM_BYTES)
    hbm, vmem = pl.BlockSpec(memory_space=pltpu.HBM), pl.BlockSpec(memory_space=pltpu.VMEM)
    like = jax.ShapeDtypeStruct

    chunks = 4
    rotated, peaks, matrix = pl.pallas_call(
        rotate_kernel,
        in_specs=[hbm] * 3,
        out_specs=[vmem] * 3,
        out_shape=[
            like((rows, width), F32),
            like((len(plane[0]), LANES), F32),
            like((FOLD, FOLD), BF16),
        ],
        scratch_shapes=[
            pltpu.VMEM((rows, width), F32),
            pltpu.VMEM((rows, width), jnp.int32),
            pltpu.VMEM((rows, width), F32),
            pltpu.SemaphoreType.DMA((chunks, 3)),
        ],
        compiler_params=pltpu.CompilerParams(vmem_limit_bytes=ROTATE_BYTES),
        name="rotate",
    )(gradient[0], sign_flips, residual[0])
    peaks = grouped(peaks, ("dp", "fsdp"), plane)
    peaks = jnp.broadcast_to(jnp.max(peaks, axis=0, keepdims=True), (depth, LANES))
    peaks = grouped(peaks, "dp", line)

    codes, full, scale, factor = pl.pallas_call(
        functools.partial(quantize_kernel, replicas),
        in_specs=[vmem] * 3,
        out_specs=[vmem] * 4,
        out_shape=[
            like((rows, width), BF16),
            like((rows, width), F32),
            like((8, LANES), F32),
            like((1, width), F32),
        ],
        scratch_shapes=[pltpu.VMEM((levels, 8, LANES), F32)] * 2,
        compiler_params=params(),
        name="quantize",
    )(peaks, rotated, level_table.reshape(1, levels))

    block = 96
    tile = pl.BlockSpec((block, width), lambda i: (i, 0))
    new_residual = pl.pallas_call(
        residual_kernel,
        grid=(rows // block,),
        in_specs=[tile, tile, pl.BlockSpec((8, LANES), lambda i: (0, 0))],
        out_specs=tile,
        out_shape=like((rows, width), F32),
        compiler_params=params(),
        cost_estimate=pl.CostEstimate(flops=2 * rows * width, bytes_accessed=12 * rows * width, transcendentals=0),
        name="residual",
    )(rotated, full, scale)

    first, second, third = len(near[0]), len(far[0]), len(half[0])
    share = rows // first
    codes = grouped(codes.reshape(first, share, width), "dp", near)
    partial = pl.pallas_call(
        functools.partial(partial_kernel, chunk_of),
        out_shape=like((second, share, width // third), F32),
        compiler_params=params(),
        name="partial",
    )(codes, matrix)
    partial = grouped(partial.astype(F16), "dp", far)
    partial, new_residual = lax.optimization_barrier((partial, new_residual))
    mean = jnp.sum(partial.astype(F32), axis=0) * 0.125
    mean = jnp.broadcast_to(mean.astype(F16)[None], (third,) + mean.shape)
    mean = grouped(mean, "dp", half)
    mean = mean.transpose(1, 0, 2).reshape(share, width)
    mean = grouped(jnp.broadcast_to(mean[None], (first, share, width)), "dp", near)
    mean = mean.reshape(rows, width).astype(F32) * factor * sign_flips.astype(F32)
    return mean, new_residual[None]


def solution(mesh):
    placed = (P("dp", "fsdp", None), P("dp", "fsdp", None), P("fsdp", None), P())
    return jax.shard_map(
        on_device,
        mesh=mesh,
        in_specs=placed,
        out_specs=(P("fsdp", None), P("dp", "fsdp", None)),
        check_vma=False,
    )
```

```python
import functools
import math

import jax
import jax.numpy as jnp
from jax import lax
from jax.experimental import pallas as pl
from jax.experimental.pallas import tpu as pltpu
from jax.sharding import PartitionSpec as P

F32, BF16, F16 = jnp.float32, jnp.bfloat16, jnp.float16
FOLD = 256
LANES = 128
VMEM_BYTES = 32 * 1024 * 1024
ROTATE_BYTES = 52 * 1024 * 1024
LOG2E = math.log2(math.e)


def hadamard(width):
    row = lax.broadcasted_iota(jnp.int32, (width, width), 0)
    col = lax.broadcasted_iota(jnp.int32, (width, width), 1)
    common = row & col
    step = 1
    while step < width.bit_length():
        common = common ^ (common >> step)
        step *= 2
    return (1 - 2 * (common & 1)).astype(F32).astype(BF16)


def butterflies(values):
    count = values.shape[1] // FOLD
    parts = [values[:, k * FOLD : (k + 1) * FOLD] for k in range(count)]
    step = 1
    while step < count:
        nxt = list(parts)
        for k in range(count):
            if not k & step:
                nxt[k] = parts[k] + parts[k + step]
                nxt[k + step] = parts[k] - parts[k + step]
        parts = nxt
        step *= 2
    return parts


def turn(part, matrix):
    high = part.astype(BF16)
    rest = part - high.astype(F32)
    middle = rest.astype(BF16)
    low = (rest - middle.astype(F32)).astype(BF16)
    dot = functools.partial(jnp.dot, preferred_element_type=F32)
    return dot(high, matrix) + (dot(middle, matrix) + dot(low, matrix))


def rotate_kernel(
    grad_hbm, flip_hbm, resid_hbm, rot_ref, peak_ref, matrix_ref,
    grad, flip, resid, sems,
):
    rows, width = rot_ref.shape
    chunks = sems.shape[0]
    deep = rows // chunks
    copies = []
    for c in range(chunks):
        at = pl.ds(c * deep, deep)
        copies.append([])
        for k, (src, dst) in enumerate(((grad_hbm, grad), (flip_hbm, flip), (resid_hbm, resid))):
            copies[c].append(pltpu.make_async_copy(src.at[at], dst.at[at], sems.at[c, k]))
            copies[c][k].start()

    matrix_ref[...] = hadamard(FOLD)

    top = jnp.zeros((8, LANES), F32)
    for c in range(chunks):
        for copy in copies[c]:
            copy.wait()
        at = slice(c * deep, (c + 1) * deep)
        signed = grad[at, :] * flip[at, :].astype(F32)
        for k, part in enumerate(butterflies(signed * (1.0 / math.sqrt(width)))):
            cols = slice(k * FOLD, (k + 1) * FOLD)
            rotated = turn(part, matrix_ref[...]) + resid[at, cols]
            rot_ref[at, cols] = rotated
            size = jnp.abs(rotated)
            for lane in range(0, FOLD, LANES):
                tiles = size[:, lane : lane + LANES].reshape(-1, 8, LANES)
                top = jnp.maximum(top, jnp.max(tiles, axis=0))
    peak_ref[...] = jnp.broadcast_to(jnp.max(top, axis=0, keepdims=True), peak_ref.shape)


def quantize_kernel(
    replicas, peaks_ref, rot_ref, level_ref, code_ref, full_ref, scale_ref, factor_ref, centre_ref, lift_ref
):
    count = level_ref.shape[1]
    levels = level_ref[...].astype(F32)
    bottom, upper = levels[:, 0:1], levels[:, count - 1 : count]
    centred = levels - (bottom + upper) * 0.5
    lift = centred * centred * (-LOG2E / 72.0)
    for k in range(count):
        centre_ref[k] = jnp.broadcast_to(centred[:, k : k + 1], (8, LANES))
        lift_ref[k] = jnp.broadcast_to(lift[:, k : k + 1], (8, LANES))
    rows, width = rot_ref.shape
    top = jnp.max(peaks_ref[...], axis=0, keepdims=True)
    peak = jnp.max(top, axis=1, keepdims=True) + 1e-06
    peak = jnp.broadcast_to(peak, (8, LANES))
    half_span = (centre_ref[count - 1] - centre_ref[0]) * 0.5
    scale = peak / half_span
    scale_ref[...] = scale
    factor_ref[...] = jnp.tile(scale[0:1] * (8.0 / replicas), (1, width // LANES))
    reach = half_span / peak * (LOG2E / 36.0)
    groups = [(r, slice(l * LANES, (l + 1) * LANES)) for l in range(width // LANES) for r in range(2)]

    def chunk(step, carry):
        row = pl.multiple_of(step * 16, 16)
        place = [rot_ref[pl.ds(row + 8 * r, 8), l] * reach for r, l in groups]
        numer, denom = [None] * len(groups), [None] * len(groups)
        for k in range(count):
            centred, lift = centre_ref[k], lift_ref[k]
            for i in range(len(groups)):
                weight = jnp.exp2(place[i] * centred + lift)
                moment = weight * centred
                numer[i] = moment if k == 0 else numer[i] + moment
                denom[i] = weight if k == 0 else denom[i] + weight
        for i in range(0, len(groups), 2):
            code = jnp.concatenate([numer[i] / denom[i], numer[i + 1] / denom[i + 1]], axis=0)
            full_ref[pl.ds(row, 16), groups[i][1]] = code
            code_ref[pl.ds(row, 16), groups[i][1]] = code.astype(BF16)
        return carry

    lax.fori_loop(0, rows // 16, chunk, 0, unroll=2)


def residual_kernel(rot_ref, full_ref, scale_ref, out_ref):
    scale = scale_ref[0:1, 0:1]
    out_ref[...] = rot_ref[...] - full_ref[...] * scale


def partial_kernel(chunk_of, codes_ref, matrix_ref, out_ref):
    width = codes_ref.shape[2]
    total = codes_ref[0].astype(F32)
    for k in range(1, codes_ref.shape[0]):
        total = total + codes_ref[k].astype(F32)
    parts = butterflies(total * (1.0 / math.sqrt(width)))
    turned = turn(jnp.concatenate(parts, axis=0), matrix_ref[...])
    chunks = jnp.split(turned, len(parts), axis=0)
    for i, chunk in enumerate(chunk_of):
        out_ref[i] = chunks[chunk]


def grouped(pieces, axes, groups):
    return lax.all_to_all(pieces, axes, 0, 0, axis_index_groups=groups)


def on_device(gradient, residual, sign_flips, level_table):
    _, rows, width = gradient.shape
    levels = level_table.shape[0]
    replicas, splits = lax.axis_size("dp"), lax.axis_size("fsdp")
    depth = 16
    ys, pairs = range(replicas // depth), range(depth // 2)
    def by_distance(lead):
        return sorted(range(depth), key=lambda z: (z != lead, -min((z - lead) % depth, (lead - z) % depth)))

    far_ring = by_distance(8)
    near = [[y * depth + 2 * h + l for y in (2, 1, 3, 0) for l in range(2)] for h in pairs]
    far = [[y * depth + z + l for z in far_ring if z % 2 == 0] for y in ys for l in range(2)]
    halves = ((8, 4, 10, 6), (14, 0, 2, 12))
    half = [[y * depth + z + l for z in members] for members in halves for y in ys for l in range(2)]
    chunk_of = [members.index(z) for z in far_ring if z % 2 == 0 for members in halves if z in members]
    line = [[y * depth + z for z in by_distance(10)] for y in ys]
    spots = sorted(((y, f) for y in ys for f in range(splits)), key=lambda spot: spot != (2, 4))
    plane = [[(y * depth + z) * splits + f for y, f in spots] for z in range(depth)]
    params = functools.partial(pltpu.CompilerParams, vmem_limit_bytes=VMEM_BYTES)
    hbm, vmem = pl.BlockSpec(memory_space=pltpu.HBM), pl.BlockSpec(memory_space=pltpu.VMEM)
    like = jax.ShapeDtypeStruct

    chunks = 4
    rotated, peaks, matrix = pl.pallas_call(
        rotate_kernel,
        in_specs=[hbm] * 3,
        out_specs=[vmem] * 3,
        out_shape=[
            like((rows, width), F32),
            like((len(plane[0]), LANES), F32),
            like((FOLD, FOLD), BF16),
        ],
        scratch_shapes=[
            pltpu.VMEM((rows, width), F32),
            pltpu.VMEM((rows, width), jnp.int32),
            pltpu.VMEM((rows, width), F32),
            pltpu.SemaphoreType.DMA((chunks, 3)),
        ],
        compiler_params=pltpu.CompilerParams(vmem_limit_bytes=ROTATE_BYTES),
        name="rotate",
    )(gradient[0], sign_flips, residual[0])
    peaks = grouped(peaks, ("dp", "fsdp"), plane)
    peaks = jnp.broadcast_to(jnp.max(peaks, axis=0, keepdims=True), (depth, LANES))
    peaks = grouped(peaks, "dp", line)

    codes, full, scale, factor = pl.pallas_call(
        functools.partial(quantize_kernel, replicas),
        in_specs=[vmem] * 3,
        out_specs=[vmem] * 4,
        out_shape=[
            like((rows, width), BF16),
            like((rows, width), F32),
            like((8, LANES), F32),
            like((1, width), F32),
        ],
        scratch_shapes=[pltpu.VMEM((levels, 8, LANES), F32)] * 2,
        compiler_params=params(),
        name="quantize",
    )(peaks, rotated, level_table.reshape(1, levels))

    block = 96
    tile = pl.BlockSpec((block, width), lambda i: (i, 0))
    new_residual = pl.pallas_call(
        residual_kernel,
        grid=(rows // block,),
        in_specs=[tile, tile, pl.BlockSpec((8, LANES), lambda i: (0, 0))],
        out_specs=tile,
        out_shape=like((rows, width), F32),
        compiler_params=params(),
        cost_estimate=pl.CostEstimate(flops=2 * rows * width, bytes_accessed=12 * rows * width, transcendentals=0),
        name="residual",
    )(rotated, full, scale)

    first, second, third = len(near[0]), len(far[0]), len(half[0])
    share = rows // first
    codes = grouped(codes.reshape(first, share, width), "dp", near)
    partial = pl.pallas_call(
        functools.partial(partial_kernel, chunk_of),
        out_shape=like((second, share, width // third), F32),
        compiler_params=params(),
        name="partial",
    )(codes, matrix)
    partial = grouped(partial.astype(F16), "dp", far)
    partial, new_residual = lax.optimization_barrier((partial, new_residual))
    mean = jnp.sum(partial.astype(F32), axis=0) * 0.125
    mean = jnp.broadcast_to(mean.astype(F16)[None], (third,) + mean.shape)
    mean = grouped(mean, "dp", half)
    mean = mean.transpose(1, 0, 2).reshape(share, width)
    mean = grouped(jnp.broadcast_to(mean[None], (first, share, width)), "dp", near)
    mean = mean.reshape(rows, width).astype(F32) * factor * sign_flips.astype(F32)
    return mean, new_residual[None]


def solution(mesh):
    placed = (P("dp", "fsdp", None), P("dp", "fsdp", None), P("fsdp", None), P())
    return jax.shard_map(
        on_device,
        mesh=mesh,
        in_specs=placed,
        out_specs=(P("fsdp", None), P("dp", "fsdp", None)),
        check_vma=False,
    )
```

```python
import functools
import math

import jax
import jax.numpy as jnp
from jax import lax
from jax.experimental import pallas as pl
from jax.experimental.pallas import tpu as pltpu
from jax.sharding import PartitionSpec as P

F32, BF16, F16 = jnp.float32, jnp.bfloat16, jnp.float16
FOLD = 256
LANES = 128
VMEM_BYTES = 32 * 1024 * 1024
ROTATE_BYTES = 52 * 1024 * 1024
LOG2E = math.log2(math.e)


def hadamard(width):
    row = lax.broadcasted_iota(jnp.int32, (width, width), 0)
    col = lax.broadcasted_iota(jnp.int32, (width, width), 1)
    common = row & col
    step = 1
    while step < width.bit_length():
        common = common ^ (common >> step)
        step *= 2
    return (1 - 2 * (common & 1)).astype(F32).astype(BF16)


def butterflies(values):
    count = values.shape[1] // FOLD
    parts = [values[:, k * FOLD : (k + 1) * FOLD] for k in range(count)]
    step = 1
    while step < count:
        nxt = list(parts)
        for k in range(count):
            if not k & step:
                nxt[k] = parts[k] + parts[k + step]
                nxt[k + step] = parts[k] - parts[k + step]
        parts = nxt
        step *= 2
    return parts


def turn(part, matrix):
    high = part.astype(BF16)
    rest = part - high.astype(F32)
    middle = rest.astype(BF16)
    low = (rest - middle.astype(F32)).astype(BF16)
    dot = functools.partial(jnp.dot, preferred_element_type=F32)
    return dot(high, matrix) + (dot(middle, matrix) + dot(low, matrix))


def rotate_kernel(
    grad_hbm, flip_hbm, resid_hbm, rot_ref, peak_ref, matrix_ref,
    grad, flip, resid, sems,
):
    rows, width = rot_ref.shape
    chunks = sems.shape[0]
    deep = rows // chunks
    copies = []
    for c in range(chunks):
        at = pl.ds(c * deep, deep)
        copies.append([])
        for k, (src, dst) in enumerate(((grad_hbm, grad), (flip_hbm, flip), (resid_hbm, resid))):
            copies[c].append(pltpu.make_async_copy(src.at[at], dst.at[at], sems.at[c, k]))
            copies[c][k].start()

    matrix_ref[...] = hadamard(FOLD)

    top = jnp.zeros((8, LANES), F32)
    for c in range(chunks):
        for copy in copies[c]:
            copy.wait()
        at = slice(c * deep, (c + 1) * deep)
        signed = grad[at, :] * flip[at, :].astype(F32)
        for k, part in enumerate(butterflies(signed * (1.0 / math.sqrt(width)))):
            cols = slice(k * FOLD, (k + 1) * FOLD)
            rotated = turn(part, matrix_ref[...]) + resid[at, cols]
            rot_ref[at, cols] = rotated
            size = jnp.abs(rotated)
            for lane in range(0, FOLD, LANES):
                tiles = size[:, lane : lane + LANES].reshape(-1, 8, LANES)
                top = jnp.maximum(top, jnp.max(tiles, axis=0))
    peak_ref[...] = jnp.broadcast_to(jnp.max(top, axis=0, keepdims=True), peak_ref.shape)


def quantize_kernel(
    replicas, peaks_ref, rot_ref, level_ref, code_ref, full_ref, scale_ref, factor_ref, centre_ref, lift_ref
):
    count = level_ref.shape[1]
    levels = level_ref[...].astype(F32)
    bottom, upper = levels[:, 0:1], levels[:, count - 1 : count]
    centred = levels - (bottom + upper) * 0.5
    lift = centred * centred * (-LOG2E / 72.0)
    for k in range(count):
        centre_ref[k] = jnp.broadcast_to(centred[:, k : k + 1], (8, LANES))
        lift_ref[k] = jnp.broadcast_to(lift[:, k : k + 1], (8, LANES))
    rows, width = rot_ref.shape
    top = jnp.max(peaks_ref[...], axis=0, keepdims=True)
    peak = jnp.max(top, axis=1, keepdims=True) + 1e-06
    peak = jnp.broadcast_to(peak, (8, LANES))
    half_span = (centre_ref[count - 1] - centre_ref[0]) * 0.5
    scale = peak / half_span
    scale_ref[...] = scale
    factor_ref[...] = jnp.tile(scale[0:1] * (8.0 / replicas), (1, width // LANES))
    reach = half_span / peak * (LOG2E / 36.0)
    groups = [(r, slice(l * LANES, (l + 1) * LANES)) for l in range(width // LANES) for r in range(2)]

    def chunk(step, carry):
        row = pl.multiple_of(step * 16, 16)
        place = [rot_ref[pl.ds(row + 8 * r, 8), l] * reach for r, l in groups]
        numer, denom = [None] * len(groups), [None] * len(groups)
        for k in range(count):
            centred, lift = centre_ref[k], lift_ref[k]
            for i in range(len(groups)):
                weight = jnp.exp2(place[i] * centred + lift)
                moment = weight * centred
                numer[i] = moment if k == 0 else numer[i] + moment
                denom[i] = weight if k == 0 else denom[i] + weight
        for i in range(0, len(groups), 2):
            code = jnp.concatenate([numer[i] / denom[i], numer[i + 1] / denom[i + 1]], axis=0)
            full_ref[pl.ds(row, 16), groups[i][1]] = code
            code_ref[pl.ds(row, 16), groups[i][1]] = code.astype(BF16)
        return carry

    lax.fori_loop(0, rows // 16, chunk, 0, unroll=2)


def residual_kernel(rot_ref, full_ref, scale_ref, out_ref):
    scale = scale_ref[0:1, 0:1]
    out_ref[...] = rot_ref[...] - full_ref[...] * scale


def partial_kernel(chunk_of, codes_ref, matrix_ref, out_ref):
    width = codes_ref.shape[2]
    total = codes_ref[0].astype(F32)
    for k in range(1, codes_ref.shape[0]):
        total = total + codes_ref[k].astype(F32)
    parts = butterflies(total * (1.0 / math.sqrt(width)))
    turned = turn(jnp.concatenate(parts, axis=0), matrix_ref[...])
    chunks = jnp.split(turned, len(parts), axis=0)
    for i, chunk in enumerate(chunk_of):
        out_ref[i] = chunks[chunk]


def grouped(pieces, axes, groups):
    return lax.all_to_all(pieces, axes, 0, 0, axis_index_groups=groups)


def on_device(gradient, residual, sign_flips, level_table):
    _, rows, width = gradient.shape
    levels = level_table.shape[0]
    replicas, splits = lax.axis_size("dp"), lax.axis_size("fsdp")
    depth = 16
    ys, pairs = range(replicas // depth), range(depth // 2)
    def by_distance(lead):
        return sorted(range(depth), key=lambda z: (z != lead, -min((z - lead) % depth, (lead - z) % depth)))

    far_ring = by_distance(8)
    near = [[y * depth + 2 * h + l for y in (2, 0, 1, 3) for l in (1, 0)] for h in pairs]
    far = [[y * depth + z + l for z in far_ring if z % 2 == 0] for y in ys for l in range(2)]
    halves = ((8, 4, 10, 6), (14, 0, 2, 12))
    half = [[y * depth + z + l for z in members] for members in halves for y in ys for l in range(2)]
    chunk_of = [members.index(z) for z in far_ring if z % 2 == 0 for members in halves if z in members]
    line = [[y * depth + z for z in by_distance(10)] for y in ys]
    spots = sorted(((y, f) for y in ys for f in range(splits)), key=lambda spot: spot != (2, 4))
    plane = [[(y * depth + z) * splits + f for y, f in spots] for z in range(depth)]
    params = functools.partial(pltpu.CompilerParams, vmem_limit_bytes=VMEM_BYTES)
    hbm, vmem = pl.BlockSpec(memory_space=pltpu.HBM), pl.BlockSpec(memory_space=pltpu.VMEM)
    like = jax.ShapeDtypeStruct

    chunks = 4
    rotated, peaks, matrix = pl.pallas_call(
        rotate_kernel,
        in_specs=[hbm] * 3,
        out_specs=[vmem] * 3,
        out_shape=[
            like((rows, width), F32),
            like((len(plane[0]), LANES), F32),
            like((FOLD, FOLD), BF16),
        ],
        scratch_shapes=[
            pltpu.VMEM((rows, width), F32),
            pltpu.VMEM((rows, width), jnp.int32),
            pltpu.VMEM((rows, width), F32),
            pltpu.SemaphoreType.DMA((chunks, 3)),
        ],
        compiler_params=pltpu.CompilerParams(vmem_limit_bytes=ROTATE_BYTES),
        name="rotate",
    )(gradient[0], sign_flips, residual[0])
    peaks = grouped(peaks, ("dp", "fsdp"), plane)
    peaks = jnp.broadcast_to(jnp.max(peaks, axis=0, keepdims=True), (depth, LANES))
    peaks = grouped(peaks, "dp", line)

    codes, full, scale, factor = pl.pallas_call(
        functools.partial(quantize_kernel, replicas),
        in_specs=[vmem] * 3,
        out_specs=[vmem] * 4,
        out_shape=[
            like((rows, width), BF16),
            like((rows, width), F32),
            like((8, LANES), F32),
            like((1, width), F32),
        ],
        scratch_shapes=[pltpu.VMEM((levels, 8, LANES), F32)] * 2,
        compiler_params=params(),
        name="quantize",
    )(peaks, rotated, level_table.reshape(1, levels))

    block = 96
    tile = pl.BlockSpec((block, width), lambda i: (i, 0))
    new_residual = pl.pallas_call(
        residual_kernel,
        grid=(rows // block,),
        in_specs=[tile, tile, pl.BlockSpec((8, LANES), lambda i: (0, 0))],
        out_specs=tile,
        out_shape=like((rows, width), F32),
        compiler_params=params(),
        cost_estimate=pl.CostEstimate(flops=2 * rows * width, bytes_accessed=12 * rows * width, transcendentals=0),
        name="residual",
    )(rotated, full, scale)

    first, second, third = len(near[0]), len(far[0]), len(half[0])
    share = rows // first
    codes = grouped(codes.reshape(first, share, width), "dp", near)
    partial = pl.pallas_call(
        functools.partial(partial_kernel, chunk_of),
        out_shape=like((second, share, width // third), F32),
        compiler_params=params(),
        name="partial",
    )(codes, matrix)
    partial = grouped(partial.astype(F16), "dp", far)
    partial, new_residual = lax.optimization_barrier((partial, new_residual))
    mean = jnp.sum(partial.astype(F32), axis=0) * 0.125
    mean = jnp.broadcast_to(mean.astype(F16)[None], (third,) + mean.shape)
    mean = grouped(mean, "dp", half)
    mean = mean.transpose(1, 0, 2).reshape(share, width)
    mean = grouped(jnp.broadcast_to(mean[None], (first, share, width)), "dp", near)
    mean = mean.reshape(rows, width).astype(F32) * factor * sign_flips.astype(F32)
    return mean, new_residual[None]


def solution(mesh):
    placed = (P("dp", "fsdp", None), P("dp", "fsdp", None), P("fsdp", None), P())
    return jax.shard_map(
        on_device,
        mesh=mesh,
        in_specs=placed,
        out_specs=(P("fsdp", None), P("dp", "fsdp", None)),
        check_vma=False,
    )
```

```python
import functools
import math

import jax
import jax.numpy as jnp
from jax import lax
from jax.experimental import pallas as pl
from jax.experimental.pallas import tpu as pltpu
from jax.sharding import PartitionSpec as P

F32, BF16, F16 = jnp.float32, jnp.bfloat16, jnp.float16
FOLD = 256
LANES = 128
VMEM_BYTES = 32 * 1024 * 1024
ROTATE_BYTES = 52 * 1024 * 1024
LOG2E = math.log2(math.e)


def hadamard(width):
    row = lax.broadcasted_iota(jnp.int32, (width, width), 0)
    col = lax.broadcasted_iota(jnp.int32, (width, width), 1)
    common = row & col
    step = 1
    while step < width.bit_length():
        common = common ^ (common >> step)
        step *= 2
    return (1 - 2 * (common & 1)).astype(F32).astype(BF16)


def butterflies(values):
    count = values.shape[1] // FOLD
    parts = [values[:, k * FOLD : (k + 1) * FOLD] for k in range(count)]
    step = 1
    while step < count:
        nxt = list(parts)
        for k in range(count):
            if not k & step:
                nxt[k] = parts[k] + parts[k + step]
                nxt[k + step] = parts[k] - parts[k + step]
        parts = nxt
        step *= 2
    return parts


def turn(part, matrix):
    high = part.astype(BF16)
    rest = part - high.astype(F32)
    middle = rest.astype(BF16)
    low = (rest - middle.astype(F32)).astype(BF16)
    dot = functools.partial(jnp.dot, preferred_element_type=F32)
    return dot(high, matrix) + (dot(middle, matrix) + dot(low, matrix))


def rotate_kernel(
    grad_hbm, flip_hbm, resid_hbm, rot_ref, peak_ref, matrix_ref,
    grad, flip, resid, sems,
):
    rows, width = rot_ref.shape
    chunks = sems.shape[0]
    deep = rows // chunks
    copies = []
    for c in range(chunks):
        at = pl.ds(c * deep, deep)
        copies.append([])
        for k, (src, dst) in enumerate(((grad_hbm, grad), (flip_hbm, flip), (resid_hbm, resid))):
            copies[c].append(pltpu.make_async_copy(src.at[at], dst.at[at], sems.at[c, k]))
            copies[c][k].start()

    matrix_ref[...] = hadamard(FOLD)

    top = jnp.zeros((8, LANES), F32)
    for c in range(chunks):
        for copy in copies[c]:
            copy.wait()
        at = slice(c * deep, (c + 1) * deep)
        signed = grad[at, :] * flip[at, :].astype(F32)
        for k, part in enumerate(butterflies(signed * (1.0 / math.sqrt(width)))):
            cols = slice(k * FOLD, (k + 1) * FOLD)
            rotated = turn(part, matrix_ref[...]) + resid[at, cols]
            rot_ref[at, cols] = rotated
            size = jnp.abs(rotated)
            for lane in range(0, FOLD, LANES):
                tiles = size[:, lane : lane + LANES].reshape(-1, 8, LANES)
                top = jnp.maximum(top, jnp.max(tiles, axis=0))
    peak_ref[...] = jnp.broadcast_to(jnp.max(top, axis=0, keepdims=True), peak_ref.shape)


def quantize_kernel(
    replicas, peaks_ref, rot_ref, level_ref, code_ref, full_ref, scale_ref, factor_ref, centre_ref, lift_ref
):
    count = level_ref.shape[1]
    levels = level_ref[...].astype(F32)
    bottom, upper = levels[:, 0:1], levels[:, count - 1 : count]
    centred = levels - (bottom + upper) * 0.5
    lift = centred * centred * (-LOG2E / 72.0)
    for k in range(count):
        centre_ref[k] = jnp.broadcast_to(centred[:, k : k + 1], (8, LANES))
        lift_ref[k] = jnp.broadcast_to(lift[:, k : k + 1], (8, LANES))
    rows, width = rot_ref.shape
    top = jnp.max(peaks_ref[...], axis=0, keepdims=True)
    peak = jnp.max(top, axis=1, keepdims=True) + 1e-06
    peak = jnp.broadcast_to(peak, (8, LANES))
    half_span = (centre_ref[count - 1] - centre_ref[0]) * 0.5
    scale = peak / half_span
    scale_ref[...] = scale
    factor_ref[...] = jnp.tile(scale[0:1] * (8.0 / replicas), (1, width // LANES))
    reach = half_span / peak * (LOG2E / 36.0)
    groups = [(r, slice(l * LANES, (l + 1) * LANES)) for l in range(width // LANES) for r in range(2)]

    def chunk(step, carry):
        row = pl.multiple_of(step * 16, 16)
        place = [rot_ref[pl.ds(row + 8 * r, 8), l] * reach for r, l in groups]
        numer, denom = [None] * len(groups), [None] * len(groups)
        for k in range(count):
            centred, lift = centre_ref[k], lift_ref[k]
            for i in range(len(groups)):
                weight = jnp.exp2(place[i] * centred + lift)
                moment = weight * centred
                numer[i] = moment if k == 0 else numer[i] + moment
                denom[i] = weight if k == 0 else denom[i] + weight
        for i in range(0, len(groups), 2):
            code = jnp.concatenate([numer[i] / denom[i], numer[i + 1] / denom[i + 1]], axis=0)
            full_ref[pl.ds(row, 16), groups[i][1]] = code
            code_ref[pl.ds(row, 16), groups[i][1]] = code.astype(BF16)
        return carry

    lax.fori_loop(0, rows // 16, chunk, 0, unroll=2)


def residual_kernel(rot_ref, full_ref, scale_ref, out_ref):
    scale = scale_ref[0:1, 0:1]
    out_ref[...] = rot_ref[...] - full_ref[...] * scale


def partial_kernel(chunk_of, codes_ref, matrix_ref, out_ref):
    width = codes_ref.shape[2]
    total = codes_ref[0].astype(F32)
    for k in range(1, codes_ref.shape[0]):
        total = total + codes_ref[k].astype(F32)
    parts = butterflies(total * (1.0 / math.sqrt(width)))
    turned = turn(jnp.concatenate(parts, axis=0), matrix_ref[...])
    chunks = jnp.split(turned, len(parts), axis=0)
    for i, chunk in enumerate(chunk_of):
        out_ref[i] = chunks[chunk]


def grouped(pieces, axes, groups):
    return lax.all_to_all(pieces, axes, 0, 0, axis_index_groups=groups)


def on_device(gradient, residual, sign_flips, level_table):
    _, rows, width = gradient.shape
    levels = level_table.shape[0]
    replicas, splits = lax.axis_size("dp"), lax.axis_size("fsdp")
    depth = 16
    ys, pairs = range(replicas // depth), range(depth // 2)
    def by_distance(lead):
        return sorted(range(depth), key=lambda z: (z != lead, -min((z - lead) % depth, (lead - z) % depth)))

    far_ring = by_distance(8)
    near = [[y * depth + 2 * h + l for y in (2, 1, 3, 0) for l in range(2)] for h in pairs]
    far = [[y * depth + z + l for z in far_ring if z % 2 == 0] for y in ys for l in range(2)]
    halves = ((8, 4, 10, 6), (14, 0, 2, 12))
    half = [[y * depth + z + l for z in members] for members in halves for y in ys for l in range(2)]
    chunk_of = [members.index(z) for z in far_ring if z % 2 == 0 for members in halves if z in members]
    line = [[y * depth + z for z in by_distance(10)] for y in ys]
    spots = sorted(((y, f) for y in ys for f in range(splits)), key=lambda spot: spot != (2, 4))
    plane = [[(y * depth + z) * splits + f for y, f in spots] for z in range(depth)]
    params = functools.partial(pltpu.CompilerParams, vmem_limit_bytes=VMEM_BYTES)
    hbm, vmem = pl.BlockSpec(memory_space=pltpu.HBM), pl.BlockSpec(memory_space=pltpu.VMEM)
    like = jax.ShapeDtypeStruct

    chunks = 4
    rotated, peaks, matrix = pl.pallas_call(
        rotate_kernel,
        in_specs=[hbm] * 3,
        out_specs=[vmem] * 3,
        out_shape=[
            like((rows, width), F32),
            like((len(plane[0]), LANES), F32),
            like((FOLD, FOLD), BF16),
        ],
        scratch_shapes=[
            pltpu.VMEM((rows, width), F32),
            pltpu.VMEM((rows, width), jnp.int32),
            pltpu.VMEM((rows, width), F32),
            pltpu.SemaphoreType.DMA((chunks, 3)),
        ],
        compiler_params=pltpu.CompilerParams(vmem_limit_bytes=ROTATE_BYTES),
        name="rotate",
    )(gradient[0], sign_flips, residual[0])
    peaks = grouped(peaks, ("dp", "fsdp"), plane)
    peaks = jnp.broadcast_to(jnp.max(peaks, axis=0, keepdims=True), (depth, LANES))
    peaks = grouped(peaks, "dp", line)

    codes, full, scale, factor = pl.pallas_call(
        functools.partial(quantize_kernel, replicas),
        in_specs=[vmem] * 3,
        out_specs=[vmem] * 4,
        out_shape=[
            like((rows, width), BF16),
            like((rows, width), F32),
            like((8, LANES), F32),
            like((1, width), F32),
        ],
        scratch_shapes=[pltpu.VMEM((levels, 8, LANES), F32)] * 2,
        compiler_params=params(),
        name="quantize",
    )(peaks, rotated, level_table.reshape(1, levels))

    first, second, third = len(near[0]), len(far[0]), len(half[0])
    share = rows // first
    codes = grouped(codes.reshape(first, share, width), "dp", near)
    partial = pl.pallas_call(
        functools.partial(partial_kernel, chunk_of),
        out_shape=like((second, share, width // third), F32),
        compiler_params=params(),
        name="partial",
    )(codes, matrix)
    partial = grouped(partial.astype(F16), "dp", far)
    partial, codes_full = lax.optimization_barrier((partial, full))
    mean = jnp.sum(partial.astype(F32), axis=0) * 0.125
    mean = jnp.broadcast_to(mean.astype(F16)[None], (third,) + mean.shape)
    block = 96
    tile = pl.BlockSpec((block, width), lambda i: (i, 0))
    new_residual = pl.pallas_call(
        residual_kernel,
        grid=(rows // block,),
        in_specs=[tile, tile, pl.BlockSpec((8, LANES), lambda i: (0, 0))],
        out_specs=tile,
        out_shape=like((rows, width), F32),
        compiler_params=params(),
        cost_estimate=pl.CostEstimate(flops=2 * rows * width, bytes_accessed=12 * rows * width, transcendentals=0),
        name="residual",
    )(rotated, codes_full, scale)
    mean = grouped(mean, "dp", half)
    mean, new_residual = lax.optimization_barrier((mean, new_residual))
    mean = mean.transpose(1, 0, 2).reshape(share, width)
    mean = grouped(jnp.broadcast_to(mean[None], (first, share, width)), "dp", near)
    mean = mean.reshape(rows, width).astype(F32) * factor * sign_flips.astype(F32)
    return mean, new_residual[None]


def solution(mesh):
    placed = (P("dp", "fsdp", None), P("dp", "fsdp", None), P("fsdp", None), P())
    return jax.shard_map(
        on_device,
        mesh=mesh,
        in_specs=placed,
        out_specs=(P("fsdp", None), P("dp", "fsdp", None)),
        check_vma=False,
    )
```
